256 devices in a mesh: rows: 16 (over x_hi, y, core), cols: 16 (over z, x_lo).
Axes of the slice: x: 4 (x_hi: 2, x_lo: 2; x = x_hi * 2 + x_lo), y: 4, z: 8, core: 2. Of those that a mesh axis runs over, the one named last changes fastest.
Arguments:
- sky: float32 [512, 131072], P('rows', 'cols'), may hold values from -16 to 16
- thresholds: float32 [5], replicated, may hold values from 0.002 to 1.6
Outputs:
- denoised: float32 [512, 131072], P('rows', 'cols')
- coarse: float32 [512, 131072], P('rows', 'cols')
The draws below stay inside these ranges and needn't reach their ends.
All inputs are finite; a program needn't handle non-finite values.
Results may differ from the reference program's by a relative error of at most 0.0003.
Values sent between devices are 32-bit elements; how exact they have to be, the bound alone decides.
No kernel may reach another device: no remote copies, remote signals or barrier semaphores. Data moves between devices by JAX's collectives and lax.ppermute only.
A program may use at most 64 MiB of HBM per device.

```python
import math
import jax
import jax.numpy as jnp
from jax import lax

WIDTH = 131072
SCALES = 5
BAND_ROWS = 512


def ripple(key, position, modulus, lowest, highest):
    stride_key, offset_key = jax.random.split(key)
    stride = jax.random.randint(stride_key, (), lowest, highest, jnp.int32)
    offset = jax.random.randint(offset_key, (), 0, modulus, jnp.int32)
    turns = ((position * stride + offset) % modulus).astype(jnp.float32)
    return jnp.cos(turns * (2.0 * math.pi / modulus))


def draw_sky(key, part):
    key = jax.random.fold_in(key, 11)
    keys = jax.random.split(key, 9)
    shape = (BAND_ROWS, WIDTH)
    level = jnp.exp(jax.random.uniform(keys[0], shape, jnp.float32, jnp.log(0.2), jnp.log(2.0)))
    row_index = jnp.arange(BAND_ROWS, dtype=jnp.int32)[:, None]
    col_index = jnp.arange(WIDTH, dtype=jnp.int32)[None, :]
    row_fast = ripple(keys[1], row_index, 256, 21, 26)
    col_slow = ripple(keys[2], col_index, 4096, 2, 17)
    col_tight = ripple(keys[3], col_index, 256, 19, 21)
    row_broad = ripple(keys[4], row_index, 4096, 4, 33)
    col_middle = ripple(keys[5], col_index, 256, 12, 14)
    row_gentle = ripple(keys[6], row_index, 4096, 4, 33)
    texture = 5.0 * row_fast * col_slow + 5.0 * col_tight * row_broad + 5.0 * col_middle * row_gentle
    spread = jax.random.uniform(keys[7], shape, jnp.float32)
    sources = jnp.where(spread < 0.002, 12000.0 * spread - 12.0, 0.0)
    noise = jax.random.truncated_normal(keys[8], -5.0, 5.0, shape, jnp.float32)
    return jnp.clip(noise * level + texture + sources, -16.0, 16.0)


def draw_thresholds(key, part):
    key = jax.random.fold_in(key, 23)
    base = 0.9 * 0.45 ** jnp.arange(SCALES, dtype=jnp.float32)
    factor = jax.random.uniform(key, (SCALES,), jnp.float32, 0.5, 1.5)
    return base * factor


def setup_inputs(seed: int = 0) -> dict:
    splits = jax.random.split(jax.random.key(seed), 3)
    return {
        "sky": draw_sky(jax.random.fold_in(splits[2], 71), 0),
        "thresholds": draw_thresholds(jax.random.fold_in(splits[2], 71), 0),
    }


def smooth(values, dilation, axis):
    reach = 2 * dilation
    spec = [(0, 0), (0, 0)]
    spec[axis] = (reach, reach)
    padded = jnp.pad(values, spec, mode="symmetric")
    count = values.shape[axis]
    weights = (1.0, 4.0, 6.0, 4.0, 1.0)
    total = jnp.zeros_like(values)
    for step in range(5):
        begin = step * dilation
        total = total + weights[step] * lax.slice_in_dim(padded, begin, begin + count, axis=axis)
    return total / 16.0


def reference(sky, thresholds):
    plane = sky
    summed = jnp.zeros_like(sky)
    for scale in range(SCALES):
        dilation = 2 ** scale
        following = smooth(smooth(plane, dilation, 1), dilation, 0)
        detail = plane - following
        summed = summed + jnp.sign(detail) * jnp.maximum(jnp.abs(detail) - thresholds[scale], 0.0)
        plane = following
    return summed + plane, plane
```

```python
import functools

import jax
import jax.numpy as jnp
from jax import lax
from jax.experimental import pallas as pl
from jax.experimental.pallas import tpu as pltpu
from jax.sharding import PartitionSpec as P

LANES = 128
TILE = 8
VMEM_LIMIT = 48 * 1024 * 1024


def swaps(count, first):
    return [(i, j) for k in range(first, count - 1, 2) for i, j in ((k, k + 1), (k + 1, k))]


def smooth_blocks(src, dst, src_base, dst_base, begin, rows, dilation, blocks, emit):
    lane = lax.broadcasted_iota(jnp.int32, (rows, LANES), 1)
    far = 2 * dilation
    keep_left = lane < LANES - far
    keep_far = lane >= far
    keep_near = lane >= dilation

    def down(block):
        def tap(step):
            return src[block, pl.ds(begin - src_base + step * dilation, rows), :]

        return (tap(-2) + tap(2)) + 4.0 * (tap(-1) + tap(1)) + 6.0 * tap(0)

    def one(block, carry, last):
        here, here_left, near_before, far_before = carry
        if last:
            after, after_left = here, here_left
        else:
            after = down(block + 1)
            after_left = pltpu.roll(after, LANES - far, 1)
        pair = here + jnp.where(keep_left, here_left, after_left)
        near = pltpu.roll(pair, dilation, 1)
        distant = pltpu.roll(pair, far, 1)
        total = (pair + jnp.where(keep_far, distant, far_before)) + 4.0 * (
            jnp.where(keep_near, near, near_before) + here
        )
        total = total * (1.0 / 256.0)
        if dst is not None:
            dst[block, pl.ds(begin - dst_base, rows), :] = total
        emit(block, total)
        return after, after_left, near, distant

    start = down(0)
    zero = jnp.zeros((rows, LANES), jnp.float32)
    carry = (start, pltpu.roll(start, LANES - far, 1), zero, zero)
    carry = lax.fori_loop(0, blocks - 1, lambda b, c: one(b, c, False), carry, unroll=5)
    one(blocks - 1, carry, True)


def nothing(block, total):
    return None


def place_rows(ext, even_in, odd_in, work, sems, blocks, tile_rows):
    index = lax.axis_index("rows")
    last = lax.axis_size("rows") - 1
    parity = index % 2
    even_at = pl.multiple_of((1 - parity) * 2 * tile_rows, TILE)
    odd_at = pl.multiple_of(parity * 2 * tile_rows, TILE)
    own = pltpu.make_async_copy(ext, work.at[:, pl.ds(tile_rows, tile_rows), :], sems.at[0])
    one = pltpu.make_async_copy(even_in, work.at[:, pl.ds(even_at, tile_rows), :], sems.at[1])
    two = pltpu.make_async_copy(odd_in, work.at[:, pl.ds(odd_at, tile_rows), :], sems.at[2])
    own.start()
    one.start()
    two.start()
    own.wait()
    one.wait()
    two.wait()

    def flip(to):
        def body(block, carry):
            for k in range(tile_rows):
                work[block, pl.ds(to + tile_rows - 1 - k, 1), :] = work[block, pl.ds(tile_rows + k, 1), :]
            return carry

        lax.fori_loop(0, blocks, body, 0)

    @pl.when(index == 0)
    def _():
        flip(0)

    @pl.when(index == last)
    def _():
        flip(2 * tile_rows)


def fine_kernel(blocks, tile_rows, levels, ext, even_in, odd_in, plane_out, cut_out, work, other, sems):
    place_rows(ext, even_in, odd_in, work, sems, blocks, tile_rows)
    own = pl.ds(tile_rows, tile_rows)

    def clipped(source, scale):
        level = levels[scale]

        def emit(block, total, first=False):
            detail = source(block) - total
            cut = jnp.minimum(jnp.maximum(detail, -level), level)
            if scale == 0:
                cut_out[block] = cut
            else:
                cut_out[block] = cut_out[block] + cut

        return emit

    def run(src, dst, src_base, dst_base, dilation, spans, scale):
        for begin, rows in spans:
            if begin == tile_rows and rows == tile_rows:
                emit = clipped(lambda b: src[b, pl.ds(tile_rows - src_base, tile_rows), :], scale)
            else:
                emit = nothing
            smooth_blocks(src, dst, src_base, dst_base, begin, rows, dilation, blocks, emit)

    t = tile_rows
    run(work, other, 0, 4, 1, ((4, t - 4), (t, t), (2 * t, t - 4)), 0)
    run(other, work, 4, 0, 2, ((8, t - 8), (t, t), (2 * t, t - 8)), 1)
    run(work, other, 0, 4, 4, ((16, t - 16), (t, t), (2 * t, t - 16)), 2)
    run(other, plane_out, 4, t, 8, ((t, t),), 3)


def coarse_kernel(blocks, tile_rows, levels, plane, even_in, odd_in, cut, sky, denoised, coarse, work, sems):
    place_rows(plane, even_in, odd_in, work, sems, blocks, tile_rows)
    level = levels[4]

    def emit(block, total):
        detail = work[block, pl.ds(tile_rows, tile_rows), :] - total
        all_cut = cut[block] + jnp.minimum(jnp.maximum(detail, -level), level)

        @pl.when(jnp.logical_and(block >= 1, block <= blocks - 2))
        def _():
            columns = pl.ds(pl.multiple_of((block - 1) * LANES, LANES), LANES)
            coarse[:, columns] = total
            denoised[:, columns] = sky[:, columns] - all_cut

    smooth_blocks(work, None, 0, 0, tile_rows, tile_rows, 16, blocks, emit)


def on_device(sky, thresholds):
    rows, columns = sky.shape
    row_count, col_count = lax.axis_size("rows"), lax.axis_size("cols")
    col = lax.axis_index("cols")
    blocks = columns // LANES + 2
    even_col = col % 2 == 0
    left_edge, right_edge = sky[:, :LANES], sky[:, columns - LANES :]
    first = lax.ppermute(jnp.where(even_col, right_edge, left_edge), "cols", swaps(col_count, 0))
    second = lax.ppermute(jnp.where(even_col, left_edge, right_edge), "cols", swaps(col_count, 1))
    left = jnp.where(even_col, second, first)
    right = jnp.where(even_col, first, second)
    left = jnp.where(col == 0, jnp.flip(left_edge, 1), left)
    right = jnp.where(col == col_count - 1, jnp.flip(right_edge, 1), right)
    inner = sky.reshape(rows, columns // LANES, LANES).transpose(1, 0, 2)
    ext = jnp.concatenate([left[None], inner, right[None]], axis=0)

    def exchange(values):
        return (
            lax.ppermute(values, "rows", swaps(row_count, 0)),
            lax.ppermute(values, "rows", swaps(row_count, 1)),
        )

    any_space = pl.BlockSpec(memory_space=pl.ANY)
    in_vmem = pl.BlockSpec(memory_space=pltpu.VMEM)
    in_smem = pl.BlockSpec(memory_space=pltpu.SMEM)
    block_shape = jax.ShapeDtypeStruct((blocks, rows, LANES), jnp.float32)
    work = pltpu.VMEM((blocks, 3 * rows, LANES), jnp.float32)
    params = pltpu.CompilerParams(vmem_limit_bytes=VMEM_LIMIT)

    plane, cut = pl.pallas_call(
        functools.partial(fine_kernel, blocks, rows),
        out_shape=(block_shape, block_shape),
        in_specs=[in_smem, any_space, any_space, any_space],
        out_specs=(in_vmem, in_vmem),
        scratch_shapes=[work, work, pltpu.SemaphoreType.DMA((3,))],
        compiler_params=params,
        name="fine",
    )(thresholds, ext, *exchange(ext))

    flat = jax.ShapeDtypeStruct((rows, columns), jnp.float32)
    return pl.pallas_call(
        functools.partial(coarse_kernel, blocks, rows),
        out_shape=(flat, flat),
        in_specs=[in_smem, any_space, any_space, any_space, in_vmem, in_vmem],
        out_specs=(in_vmem, in_vmem),
        scratch_shapes=[work, pltpu.SemaphoreType.DMA((3,))],
        compiler_params=params,
        name="coarse",
    )(thresholds, plane, *exchange(plane), cut, sky)


def solution(mesh):
    return jax.shard_map(
        on_device,
        mesh=mesh,
        in_specs=(P("rows", "cols"), P()),
        out_specs=(P("rows", "cols"), P("rows", "cols")),
        check_vma=False,
    )
```

```python
import functools

import jax
import jax.numpy as jnp
import ml_dtypes
import numpy as np
from jax import lax
from jax.experimental import pallas as pl
from jax.experimental.pallas import tpu as pltpu
from jax.sharding import PartitionSpec as P

LANES = 128
HALF = LANES // 2
PAIR = 2 * LANES
SPAN = PAIR + LANES
TILE = 8
SCALES = 5
MEBI = 1024 * 1024
BATCH = 16
F32, BF16 = jnp.float32, jnp.bfloat16


def swaps(count, first):
    return [(i, j) for k in range(first, count - 1, 2) for i, j in ((k, k + 1), (k + 1, k))]


def column_weights(scales):
    taps = np.ones(1)
    for scale in range(scales):
        step = np.zeros(4 * 2**scale + 1)
        step[:: 2**scale] = (1.0, 4.0, 6.0, 4.0, 1.0)
        taps = np.convolve(taps, step)
    reach = len(taps) // 2
    source = np.concatenate([np.arange(PAIR + HALF), np.arange(-HALF, 0)])
    offset = source[:, None] - np.arange(PAIR)[None, :]
    exact = np.where(np.abs(offset) <= reach, taps[np.clip(offset + reach, 0, 2 * reach)], 0.0) * 2.0 ** (-8 * scales)
    high = exact.astype(ml_dtypes.bfloat16)
    low = (exact - high.astype(np.float64)).astype(ml_dtypes.bfloat16)
    return [high, low] if np.any(low.astype(np.float32)) else [high]


def binomial(a, b, c, d, e):
    return (a + e) + 4.0 * (b + d) + 6.0 * c


def columns_of(block, width=LANES):
    if isinstance(block, int):
        return slice(block * width, (block + 1) * width)
    return pl.ds(pl.multiple_of(block * width, width), width)


def loop(begin, end, body, group=1):
    def step(k, carry):
        for slot in range(group):
            body(begin + k * group + slot, slot)
        return carry

    whole = (end - begin) // group
    lax.fori_loop(0, whole, step, 0)
    for index in range(begin + whole * group, end):
        body(index, index - begin - whole * group)


def with_neighbours(own, odd_in, flipped, run):
    rows = own[0].shape[0]
    index, last = lax.axis_index("rows"), lax.axis_size("rows") - 1
    outer = jnp.logical_or(index == 0, index == last)

    @pl.when(outer)
    def _():
        for source, target in zip(own, flipped):
            for k in range(rows):
                target[k : k + 1, :] = source[rows - 1 - k : rows - k, :]
        run(flipped)

    @pl.when(jnp.logical_not(outer))
    def _():
        run(odd_in)


def load_block(own, even, odd, buffer):
    rows = own.shape[0]
    parity = lax.axis_index("rows") % 2
    buffer[rows : 2 * rows, :] = own
    buffer[pl.ds(pl.multiple_of((1 - parity) * 2 * rows, TILE), rows), :] = even
    buffer[pl.ds(pl.multiple_of(parity * 2 * rows, TILE), rows), :] = odd


def taps(buffer, begin, step, count):
    return [buffer[begin + k * step : begin + k * step + count, :] for k in (-2, -1, 0, 1, 2)]


def take_kernel(sky, part, first, second):
    columns = sky.shape[1]
    part[...] = sky[:, 0 : part.shape[1]]
    left, right = sky[:, 0:LANES], sky[:, columns - LANES : columns]
    even = lax.axis_index("cols") % 2 == 0
    first[...] = jnp.where(even, right, left)
    second[...] = jnp.where(even, left, right)


def join_kernel(sky, first, second, rest):
    width, columns = rest.shape[1] - LANES, sky.shape[1]
    rest[:, 0:width] = sky[:, columns - width : columns]
    rows = sky.shape[0]
    index, last = lax.axis_index("cols"), lax.axis_size("cols") - 1
    in_first = lax.broadcasted_iota(jnp.int32, (rows, LANES), 1) < HALF
    even = index % 2 == 0
    left = jnp.where(even, second[...], first[...])
    right = jnp.where(even, first[...], second[...])
    halo = slice(width, width + LANES)
    rest[:, halo] = jnp.where(in_first, right, left)

    def flip(value):
        row = lax.broadcasted_iota(jnp.int32, (LANES, LANES), 0)
        lane = lax.broadcasted_iota(jnp.int32, (LANES, LANES), 1)
        turn = (row + lane == LANES - 1).astype(F32)
        return jnp.dot(value, turn, preferred_element_type=F32, precision=lax.Precision.HIGHEST)

    @pl.when(index == 0)
    def _():
        rest[:, halo] = jnp.where(in_first, right, flip(sky[:, 0:LANES]))

    @pl.when(index == last)
    def _():
        rest[:, halo] = jnp.where(in_first, flip(sky[:, columns - LANES : columns]), left)


def rows_kernel(group, own, even_in, odd_in, out, flipped, *buffers):
    rows = own.shape[0]

    def run(odd):
        def one(block, slot):
            zero, ones, twos = buffers[3 * slot : 3 * slot + 3]
            columns = columns_of(block)
            load_block(own[:, columns], even_in[:, columns], odd[0][:, columns], zero)
            ones[...] = binomial(*taps(zero, 4, 1, 3 * rows - 8))
            two = binomial(*taps(ones, 4, 2, 3 * rows - 16))
            twos[...] = two
            n = 3 * rows - 32
            three = binomial(two[0:n], twos[4 : n + 4, :], two[8 : n + 8], twos[12 : n + 12, :], two[16 : n + 16])
            out[:, columns] = binomial(*[three[8 * k : 8 * k + rows] for k in range(5)])

        loop(0, own.shape[1] // LANES, one, group)

    with_neighbours((own,), (odd_in,), (flipped,), run)


def put(value, operand, rows, main=None, after=None, before=None):
    high = value.astype(BF16)
    low = (value - high.astype(F32)).astype(BF16)

    def at(slot):
        return slice(slot * rows, (slot + 1) * rows) if isinstance(slot, int) else pl.ds(pl.multiple_of(slot * rows, 16), rows)

    for base, piece in ((0, high), (SPAN, low)):
        if main is not None:
            operand[at(main[0]), base + main[1] * LANES : base + (main[1] + 1) * LANES] = piece
        if after is not None:
            operand[at(after), base + PAIR : base + PAIR + HALF] = piece[:, :HALF]
        if before is not None:
            operand[at(before), base + PAIR + HALF : base + SPAN] = piece[:, HALF:]


def clip(detail, level):
    return jnp.minimum(jnp.maximum(detail, -level), level)


def filter_columns(operand, weights, rows, start, count, emit):
    value = operand[start * rows : (start + count) * rows, :]
    total = None
    for weight in weights:
        term = jnp.dot(value[:, : weight.shape[0]], weight[...], preferred_element_type=F32)
        total = term if total is None else total + term
    for k in range(count):
        emit(start + k, total[k * rows : (k + 1) * rows])


def details_kernel(pairs, weight_counts, levels, *refs):
    own, even_in, odd_in, four, refs = refs[:2], refs[2:4], refs[4:6], refs[6:8], refs[8:]
    weights, refs = refs[: sum(weight_counts)], refs[sum(weight_counts) :]
    out, plane, refs = refs[0], refs[1], refs[2:]
    flipped, operands, buffers = refs[:2], refs[2:6], refs[6:]
    rows = own[0].shape[0]
    first = own[0].shape[1] // PAIR

    def run(odd):
        def one(span, block, slot):
            zero, ones, twos = buffers[3 * slot : 3 * slot + 3]
            columns = columns_of(block)
            load_block(own[span][:, columns], even_in[span][:, columns], odd[span][:, columns], zero)
            ones[...] = binomial(*taps(zero, rows - 12, 1, rows + 24))
            two = binomial(*taps(ones, 4, 2, rows + 16))
            twos[...] = two
            three = binomial(two[0:rows], twos[4 : rows + 4, :], two[8 : rows + 8], twos[12 : rows + 12, :], two[16 : rows + 16])
            return ones[12 : rows + 12, :], two[8 : rows + 8], three, four[span][:, columns]

        for span, begin, end in ((0, 0, first), (1, first, pairs)):

            def body(pair, _):
                block = 2 * (pair - begin)
                left, right = one(span, block, 0), one(span, block + 1, 1)
                for k in range(4):
                    put(left[k], operands[k], rows, main=(pair + 1, 0), after=pair)
                    put(right[k], operands[k], rows, main=(pair + 1, 1), before=pair + 2)

            loop(begin, end, body)
        for k, value in enumerate(one(1, 2 * (pairs - first), 0)):
            put(value, operands[k], rows, after=pairs, before=1)

    with_neighbours(own, odd_in, flipped, run)

    at = 0
    for scale in range(4):
        use = weights[at : at + weight_counts[scale]]
        at += weight_counts[scale]
        level = levels[scale]

        def emit(slot, total):
            pair = slot - 1
            columns = columns_of(pair, PAIR)
            if scale == 0:
                sky = own[0][:, columns] if pair < first else own[1][:, columns_of(pair - first, PAIR)]
                out[:, columns] = sky - clip(sky - total, level)
            else:
                out[:, columns] = out[:, columns] - clip(plane[:, columns] - total, level)
            plane[:, columns] = total

        for start in range(0, pairs, BATCH):
            filter_columns(operands[scale], use, rows, start + 1, BATCH, emit)


def last_rows(own, even_in, odd, then):
    half = own[0].shape[0] // 2

    def with_sides(above, below):
        def one(span, block):
            columns = columns_of(block)
            a, b = above[span][0:half, columns], above[span][half : 2 * half, columns]
            c, d = own[span][0:half, columns], own[span][half : 2 * half, columns]
            e, f = below[span][0:half, columns], below[span][half : 2 * half, columns]
            return jnp.concatenate([binomial(a, b, c, d, e), binomial(b, c, d, e, f)], axis=0)

        then(one)

    parity = lax.axis_index("rows") % 2
    pl.when(parity == 0)(lambda: with_sides(odd, even_in))
    pl.when(parity == 1)(lambda: with_sides(even_in, odd))


def finish(operand, weights, rows, start, count, level, pair_of, part_sum, plane, denoised, coarse):
    def emit(slot, total):
        columns, place = columns_of(pair_of(slot), PAIR), columns_of(slot - start, PAIR)
        coarse[:, place] = total
        denoised[:, place] = part_sum[:, columns] - clip(plane[:, columns] - total, level)

    filter_columns(operand, weights, rows, start, count, emit)


def row_copies(source, target, begin, sems):
    columns = slice(begin, begin + source.shape[1])
    return [
        pltpu.make_async_copy(source.at[row : row + TILE, :], target.at[row : row + TILE, columns], sems.at[k])
        for k, row in enumerate(range(0, source.shape[0], TILE))
    ]


def coarse_one_kernel(levels, own, even_in, odd_in, part_sum, plane, high, low, denoised, coarse, flipped, operand):
    rows = own.shape[0]
    pairs = own.shape[1] // PAIR

    def blocks(one):
        def body(pair, _):
            put(one(0, 2 * pair), operand, rows, main=(pair, 0), after=pair - 1)
            put(one(0, 2 * pair + 1), operand, rows, main=(pair, 1), before=pair + 1)

        put(one(0, 1), operand, rows, before=1)
        loop(1, pairs - 1, body)
        put(one(0, 2 * pairs - 2), operand, rows, after=pairs - 2)

    with_neighbours((own,), (odd_in,), (flipped,), lambda odd: last_rows((own,), (even_in,), odd, blocks))
    finish(operand, (high, low), rows, 1, pairs - 2, levels[4], lambda slot: slot, part_sum, plane, denoised, coarse)


def coarse_two_kernel(levels, *refs):
    own, even_in, odd_in, refs = refs[:2], refs[2:4], refs[4:6], refs[6:]
    part_sum, plane, high, low, den_one, coa_one, denoised, coarse, *refs = refs
    flipped, (operand, den_two, coa_two, den_three, coa_three, sems) = refs[:2], refs[2:]
    rows, columns = part_sum.shape
    first, pairs = own[0].shape[1] // PAIR, columns // PAIR
    begin = first - 1
    copies = row_copies(den_one, denoised, PAIR, sems.at[0]) + row_copies(coa_one, coarse, PAIR, sems.at[1])
    for copy in copies:
        copy.start()

    def blocks(one):
        def body(pair, _):
            block = 2 * (pair - first)
            put(one(1, block), operand, rows, main=(pair - begin + 1, 0), after=pair - begin)
            put(one(1, block + 1), operand, rows, main=(pair - begin + 1, 1), before=pair - begin + 2)

        loop(first, pairs, body)
        put(one(0, 2 * begin), operand, rows, main=(1, 0))
        put(one(0, 2 * begin + 1), operand, rows, main=(1, 1), before=2)
        put(one(0, 2 * begin - 1), operand, rows, before=1)
        put(one(1, 2 * (pairs - first)), operand, rows, after=pairs - begin, before=0)
        put(one(0, 0), operand, rows, main=(0, 0))
        put(one(0, 1), operand, rows, main=(0, 1))
        put(one(0, 2), operand, rows, after=0)

    with_neighbours(own, odd_in, flipped, lambda odd: last_rows(own, even_in, odd, blocks))
    count = pairs - begin + 1
    half = count // 2
    pair_of = lambda slot: slot + begin - 1 if slot else 0
    for start, size, den, coa, at in ((0, half, den_two, coa_two, 2), (half, count - half, den_three, coa_three, 6)):
        finish(operand, (high, low), rows, start, size, levels[4], pair_of, part_sum, plane, den, coa)
        for source, target, k in ((den, denoised, at), (coa, coarse, at + 1)):
            if start == 0:
                more = row_copies(source.at[:, 0:PAIR], target, 0, sems.at[k])
                more += row_copies(source.at[:, PAIR : half * PAIR], target, begin * PAIR, sems.at[k + 2])
            else:
                more = row_copies(source, target, (begin + half - 1) * PAIR, sems.at[k])
            for copy in more:
                copy.start()
            copies += more
    for copy in copies:
        copy.wait()


def on_device(sky, thresholds):
    rows, columns = sky.shape
    row_count, col_count = lax.axis_size("rows"), lax.axis_size("cols")
    blocks, pairs = columns // LANES, columns // PAIR
    first = blocks // 2 + 2
    weights = [
        [jnp.asarray(w if k else np.concatenate([w, w])) for k, w in enumerate(column_weights(scale + 1))]
        for scale in range(SCALES)
    ]

    any_space = pl.BlockSpec(memory_space=pl.ANY)
    in_vmem = pl.BlockSpec(memory_space=pltpu.VMEM)
    in_smem = pl.BlockSpec(memory_space=pltpu.SMEM)
    dma = pltpu.SemaphoreType.DMA

    def room(mebibytes):
        return pltpu.CompilerParams(vmem_limit_bytes=mebibytes * MEBI)

    def array(width):
        return jax.ShapeDtypeStruct((rows, width), F32)

    def vmem(width):
        return pltpu.VMEM((rows, width), F32)

    def operand(slots):
        return pltpu.VMEM((slots * rows, 2 * SPAN), BF16)

    def exchange(values):
        return (
            lax.ppermute(values, "rows", swaps(row_count, 0)),
            lax.ppermute(values, "rows", swaps(row_count, 1)),
        )

    widths = (first * LANES, (blocks - first + 1) * LANES)
    part, one, two = pl.pallas_call(
        take_kernel,
        out_shape=(array(widths[0]), array(LANES), array(LANES)),
        in_specs=[in_vmem],
        out_specs=(in_vmem,) * 3,
        compiler_params=room(8),
        name="take",
    )(sky)
    near = [exchange(part)]
    one = lax.ppermute(one, "cols", swaps(col_count, 0))
    two = lax.ppermute(two, "cols", swaps(col_count, 1))
    rest = pl.pallas_call(
        join_kernel,
        out_shape=array(widths[1]),
        in_specs=[in_vmem] * 3,
        out_specs=in_vmem,
        compiler_params=room(8),
        cost_estimate=pl.CostEstimate(flops=3 * 10**10, bytes_accessed=10**6, transcendentals=0),
        name="join",
    )(sky, one, two)
    near.append(exchange(rest))
    own = (part, rest)
    group = 4

    def smooth_rows(which, name):
        width = widths[which]
        return pl.pallas_call(
            functools.partial(rows_kernel, group),
            out_shape=array(width),
            in_specs=[in_vmem] * 3,
            out_specs=in_vmem,
            scratch_shapes=[vmem(width)]
            + [pltpu.VMEM((3 * rows - cut, LANES), F32) for _ in range(group) for cut in (0, 8, 16)],
            compiler_params=room(10),
            name=name,
        )(own[which], *near[which])

    four = [smooth_rows(0, "rows_one")]
    near_four = [exchange(four[0])]
    four.append(smooth_rows(1, "rows_two"))
    near_four.append(exchange(four[1]))

    def columnwise(pairs_of_inputs):
        return [x[0] for x in pairs_of_inputs] + [x[1] for x in pairs_of_inputs]

    fine = [w for scale in range(4) for w in weights[scale]]
    part_sum, plane = pl.pallas_call(
        functools.partial(details_kernel, pairs, tuple(len(weights[scale]) for scale in range(4))),
        out_shape=(array(columns), array(columns)),
        in_specs=[in_smem] + [in_vmem] * (8 + len(fine)),
        out_specs=(in_vmem, in_vmem),
        scratch_shapes=[vmem(w) for w in widths]
        + [operand(pairs + 2)] * 4
        + [pltpu.VMEM((n, LANES), F32) for _ in range(2) for n in (3 * rows, rows + 24, rows + 16)],
        compiler_params=room(28),
        name="details",
    )(thresholds, *own, *columnwise(near), *four, *fine)

    inner = first // 2 - 2
    outs = pl.pallas_call(
        coarse_one_kernel,
        out_shape=(array(inner * PAIR),) * 2,
        in_specs=[in_smem] + [in_vmem] * 7,
        out_specs=(in_vmem,) * 2,
        scratch_shapes=[vmem(widths[0]), operand(inner + 2)],
        compiler_params=room(16),
        name="coarse_one",
    )(thresholds, four[0], *near_four[0], part_sum, plane, *weights[4])
    count = pairs - inner
    return pl.pallas_call(
        coarse_two_kernel,
        out_shape=(array(columns), array(columns)),
        in_specs=[in_smem] + [in_vmem] * 12,
        out_specs=(pl.BlockSpec(memory_space=pltpu.HBM),) * 2,
        scratch_shapes=[vmem(w) for w in widths]
        + [operand(count + 2)]
        + [vmem(n * PAIR) for n in (count // 2, count // 2, count - count // 2, count - count // 2)]
        + [dma((8, rows // TILE))],
        compiler_params=room(16),
        name="coarse_two",
    )(thresholds, *four, *columnwise(near_four), part_sum, plane, *weights[4], *outs)


def solution(mesh):
    return jax.shard_map(
        on_device,
        mesh=mesh,
        in_specs=(P("rows", "cols"), P()),
        out_specs=(P("rows", "cols"), P("rows", "cols")),
        check_vma=False,
    )
```

```python
import functools

import jax
import jax.numpy as jnp
import ml_dtypes
import numpy as np
from jax import lax
from jax.experimental import pallas as pl
from jax.experimental.pallas import tpu as pltpu
from jax.sharding import PartitionSpec as P

LANES = 128
HALF = LANES // 2
PAIR = 2 * LANES
SPAN = PAIR + LANES
TILE = 8
SCALES = 5
MEBI = 1024 * 1024
BATCH = 16
F32, BF16 = jnp.float32, jnp.bfloat16


def swaps(count, first):
    return [(i, j) for k in range(first, count - 1, 2) for i, j in ((k, k + 1), (k + 1, k))]


def column_weights(scales):
    taps = np.ones(1)
    for scale in range(scales):
        step = np.zeros(4 * 2**scale + 1)
        step[:: 2**scale] = (1.0, 4.0, 6.0, 4.0, 1.0)
        taps = np.convolve(taps, step)
    reach = len(taps) // 2
    source = np.concatenate([np.arange(PAIR + HALF), np.arange(-HALF, 0)])
    offset = source[:, None] - np.arange(PAIR)[None, :]
    exact = np.where(np.abs(offset) <= reach, taps[np.clip(offset + reach, 0, 2 * reach)], 0.0) * 2.0 ** (-8 * scales)
    high = exact.astype(ml_dtypes.bfloat16)
    low = (exact - high.astype(np.float64)).astype(ml_dtypes.bfloat16)
    return [high, low] if np.any(low.astype(np.float32)) else [high]


def binomial(a, b, c, d, e):
    return (a + e) + 4.0 * (b + d) + 6.0 * c


def columns_of(block, width=LANES):
    if isinstance(block, int):
        return slice(block * width, (block + 1) * width)
    return pl.ds(pl.multiple_of(block * width, width), width)


def loop(begin, end, body, group=1):
    def step(k, carry):
        for slot in range(group):
            body(begin + k * group + slot, slot)
        return carry

    whole = (end - begin) // group
    lax.fori_loop(0, whole, step, 0)
    for index in range(begin + whole * group, end):
        body(index, index - begin - whole * group)


def with_neighbours(own, odd_in, flipped, run, prepare=None):
    rows = own[0].shape[0]
    index, last = lax.axis_index("rows"), lax.axis_size("rows") - 1
    outer = jnp.logical_or(index == 0, index == last)

    @pl.when(outer)
    def _():
        for source, target in zip(own, flipped):
            for k in range(rows):
                target[k : k + 1, :] = source[rows - 1 - k : rows - k, :]
        run(flipped)

    @pl.when(jnp.logical_not(outer))
    def _():
        if prepare is not None:
            prepare()
        run(odd_in)


def load_block(own, even, odd, buffer):
    rows = own.shape[0]
    parity = lax.axis_index("rows") % 2
    buffer[rows : 2 * rows, :] = own
    buffer[pl.ds(pl.multiple_of((1 - parity) * 2 * rows, TILE), rows), :] = even
    buffer[pl.ds(pl.multiple_of(parity * 2 * rows, TILE), rows), :] = odd


def taps(buffer, begin, step, count):
    return [buffer[begin + k * step : begin + k * step + count, :] for k in (-2, -1, 0, 1, 2)]


def take_kernel(sky, part, first, second):
    columns = sky.shape[1]
    part[...] = sky[:, 0 : part.shape[1]]
    left, right = sky[:, 0:LANES], sky[:, columns - LANES : columns]
    even = lax.axis_index("cols") % 2 == 0
    first[...] = jnp.where(even, right, left)
    second[...] = jnp.where(even, left, right)


def join_kernel(sky, first, second, rest):
    width, columns = rest.shape[1] - LANES, sky.shape[1]
    rest[:, 0:width] = sky[:, columns - width : columns]
    rows = sky.shape[0]
    index, last = lax.axis_index("cols"), lax.axis_size("cols") - 1
    in_first = lax.broadcasted_iota(jnp.int32, (rows, LANES), 1) < HALF
    even = index % 2 == 0
    left = jnp.where(even, second[...], first[...])
    right = jnp.where(even, first[...], second[...])
    halo = slice(width, width + LANES)
    rest[:, halo] = jnp.where(in_first, right, left)

    def flip(value):
        row = lax.broadcasted_iota(jnp.int32, (LANES, LANES), 0)
        lane = lax.broadcasted_iota(jnp.int32, (LANES, LANES), 1)
        turn = (row + lane == LANES - 1).astype(F32)
        return jnp.dot(value, turn, preferred_element_type=F32, precision=lax.Precision.HIGHEST)

    @pl.when(index == 0)
    def _():
        rest[:, halo] = jnp.where(in_first, right, flip(sky[:, 0:LANES]))

    @pl.when(index == last)
    def _():
        rest[:, halo] = jnp.where(in_first, flip(sky[:, columns - LANES : columns]), left)


def smooth_tile(group, own, even_in, odd_in, out, buffers):
    rows = own.shape[0]

    def one(block, slot):
        zero, ones, twos = buffers[3 * slot : 3 * slot + 3]
        columns = columns_of(block)
        load_block(own[:, columns], even_in[:, columns], odd_in[:, columns], zero)
        ones[...] = binomial(*taps(zero, 4, 1, 3 * rows - 8))
        two = binomial(*taps(ones, 4, 2, 3 * rows - 16))
        twos[...] = two
        n = 3 * rows - 32
        three = binomial(two[0:n], twos[4 : n + 4, :], two[8 : n + 8], twos[12 : n + 12, :], two[16 : n + 16])
        out[:, columns] = binomial(*[three[8 * k : 8 * k + rows] for k in range(5)])

    loop(0, own.shape[1] // LANES, one, group)


def rows_kernel(group, own, even_in, odd_in, out, flipped, *buffers):
    def run(odd):
        smooth_tile(group, own, even_in, odd[0], out, buffers)

    with_neighbours((own,), (odd_in,), (flipped,), run)


def far_kernel(group, after, own, even_in, odd_in, *refs):
    out, *buffers = refs[after:]
    smooth_tile(group, own, even_in, odd_in, out, buffers)


def put(value, operand, rows, main=None, after=None, before=None):
    high = value.astype(BF16)
    low = (value - high.astype(F32)).astype(BF16)

    def at(slot):
        return slice(slot * rows, (slot + 1) * rows) if isinstance(slot, int) else pl.ds(pl.multiple_of(slot * rows, 16), rows)

    for base, piece in ((0, high), (SPAN, low)):
        if main is not None:
            operand[at(main[0]), base + main[1] * LANES : base + (main[1] + 1) * LANES] = piece
        if after is not None:
            operand[at(after), base + PAIR : base + PAIR + HALF] = piece[:, :HALF]
        if before is not None:
            operand[at(before), base + PAIR + HALF : base + SPAN] = piece[:, HALF:]


def clip(detail, level):
    return jnp.minimum(jnp.maximum(detail, -level), level)


def filter_columns(operand, weights, rows, start, count, emit):
    value = operand[start * rows : (start + count) * rows, :]
    total = None
    for weight in weights:
        term = jnp.dot(value[:, : weight.shape[0]], weight[...], preferred_element_type=F32)
        total = term if total is None else total + term
    for k in range(count):
        emit(start + k, total[k * rows : (k + 1) * rows])


def details_kernel(pairs, weight_counts, levels, *refs):
    own, even_in, odd_in, four, refs = refs[:2], refs[2:4], refs[4:6], refs[6:8], refs[8:]
    weights, refs = refs[: sum(weight_counts)], refs[sum(weight_counts) :]
    out, plane, refs = refs[0], refs[1], refs[2:]
    flipped, operands, buffers = refs[:2], refs[2:6], refs[6:]
    rows = own[0].shape[0]
    first = own[0].shape[1] // PAIR

    def run(odd):
        def one(span, block, slot):
            zero, ones, twos = buffers[3 * slot : 3 * slot + 3]
            columns = columns_of(block)
            load_block(own[span][:, columns], even_in[span][:, columns], odd[span][:, columns], zero)
            ones[...] = binomial(*taps(zero, rows - 12, 1, rows + 24))
            two = binomial(*taps(ones, 4, 2, rows + 16))
            twos[...] = two
            three = binomial(two[0:rows], twos[4 : rows + 4, :], two[8 : rows + 8], twos[12 : rows + 12, :], two[16 : rows + 16])
            return ones[12 : rows + 12, :], two[8 : rows + 8], three, four[span][:, columns]

        for span, begin, end in ((0, 0, first), (1, first, pairs)):

            def body(pair, _):
                block = 2 * (pair - begin)
                left, right = one(span, block, 0), one(span, block + 1, 1)
                for k in range(4):
                    put(left[k], operands[k], rows, main=(pair + 1, 0), after=pair)
                    put(right[k], operands[k], rows, main=(pair + 1, 1), before=pair + 2)

            loop(begin, end, body)
        for k, value in enumerate(one(1, 2 * (pairs - first), 0)):
            put(value, operands[k], rows, after=pairs, before=1)

    with_neighbours(own, odd_in, flipped, run)

    at = 0
    for scale in range(4):
        use = weights[at : at + weight_counts[scale]]
        at += weight_counts[scale]
        level = levels[scale]

        def emit(slot, total):
            pair = slot - 1
            columns = columns_of(pair, PAIR)
            if scale == 0:
                sky = own[0][:, columns] if pair < first else own[1][:, columns_of(pair - first, PAIR)]
                out[:, columns] = sky - clip(sky - total, level)
            else:
                out[:, columns] = out[:, columns] - clip(plane[:, columns] - total, level)
            plane[:, columns] = total

        for start in range(0, pairs, BATCH):
            filter_columns(operands[scale], use, rows, start + 1, BATCH, emit)


def last_rows(own, even_in, odd, then):
    half = own[0].shape[0] // 2

    def with_sides(above, below):
        def one(span, block):
            columns = columns_of(block)
            a, b = above[span][0:half, columns], above[span][half : 2 * half, columns]
            c, d = own[span][0:half, columns], own[span][half : 2 * half, columns]
            e, f = below[span][0:half, columns], below[span][half : 2 * half, columns]
            return jnp.concatenate([binomial(a, b, c, d, e), binomial(b, c, d, e, f)], axis=0)

        then(one)

    parity = lax.axis_index("rows") % 2
    pl.when(parity == 0)(lambda: with_sides(odd, even_in))
    pl.when(parity == 1)(lambda: with_sides(even_in, odd))


def finish(operand, weights, rows, start, count, level, pair_of, part_sum, plane, denoised, coarse):
    def emit(slot, total):
        columns, place = columns_of(pair_of(slot), PAIR), columns_of(slot - start, PAIR)
        coarse[:, place] = total
        denoised[:, place] = part_sum[:, columns] - clip(plane[:, columns] - total, level)

    filter_columns(operand, weights, rows, start, count, emit)


def row_copies(source, target, begin, sems):
    columns = slice(begin, begin + source.shape[1])
    return [
        pltpu.make_async_copy(source.at[row : row + TILE, :], target.at[row : row + TILE, columns], sems.at[k])
        for k, row in enumerate(range(0, source.shape[0], TILE))
    ]


def coarse_one_kernel(levels, own, even_in, odd_in, part_sum, plane, high, low, denoised, coarse, flipped, operand):
    rows = own.shape[0]
    pairs = own.shape[1] // PAIR

    def blocks(one):
        def body(pair, _):
            put(one(0, 2 * pair), operand, rows, main=(pair, 0), after=pair - 1)
            put(one(0, 2 * pair + 1), operand, rows, main=(pair, 1), before=pair + 1)

        put(one(0, 1), operand, rows, before=1)
        loop(1, pairs - 1, body)
        put(one(0, 2 * pairs - 2), operand, rows, after=pairs - 2)

    with_neighbours((own,), (odd_in,), (flipped,), lambda odd: last_rows((own,), (even_in,), odd, blocks))
    finish(operand, (high, low), rows, 1, pairs - 2, levels[4], lambda slot: slot, part_sum, plane, denoised, coarse)


def coarse_two_kernel(levels, *refs):
    own, even_in, refs = refs[:2], refs[2:4], refs[4:]
    far, part_sum, plane, high, low, den_one, coa_one, denoised, coarse, *refs = refs[:2], *refs[2:]
    flipped, (operand, den_two, coa_two, den_three, coa_three, sems) = refs[:2], refs[2:]
    rows, columns = part_sum.shape
    first, pairs = own[0].shape[1] // PAIR, columns // PAIR
    begin = first - 1
    copies = row_copies(den_one, denoised, PAIR, sems.at[6]) + row_copies(coa_one, coarse, PAIR, sems.at[7])
    for copy in copies:
        copy.start()

    def blocks(one):
        def body(pair, _):
            block = 2 * (pair - first)
            put(one(1, block), operand, rows, main=(pair - begin + 1, 0), after=pair - begin)
            put(one(1, block + 1), operand, rows, main=(pair - begin + 1, 1), before=pair - begin + 2)

        loop(first, pairs, body)
        put(one(0, 2 * begin), operand, rows, main=(1, 0))
        put(one(0, 2 * begin + 1), operand, rows, main=(1, 1), before=2)
        put(one(0, 2 * begin - 1), operand, rows, before=1)
        put(one(1, 2 * (pairs - first)), operand, rows, after=pairs - begin, before=0)
        put(one(0, 0), operand, rows, main=(0, 0))
        put(one(0, 1), operand, rows, main=(0, 1))
        put(one(0, 2), operand, rows, after=0)

    with_neighbours(own, far, flipped, lambda odd: last_rows(own, even_in, odd, blocks))
    count = pairs - begin + 1
    half = count // 2
    pair_of = lambda slot: slot + begin - 1 if slot else 0
    for start, size, den, coa, at in ((0, half, den_two, coa_two, 0), (half, count - half, den_three, coa_three, 4)):
        finish(operand, (high, low), rows, start, size, levels[4], pair_of, part_sum, plane, den, coa)
        for source, target, k in ((den, denoised, at), (coa, coarse, at + 1)):
            if start == 0:
                more = row_copies(source.at[:, 0:PAIR], target, 0, sems.at[k])
                more += row_copies(source.at[:, PAIR : half * PAIR], target, begin * PAIR, sems.at[k + 2])
            else:
                more = row_copies(source, target, (begin + half - 1) * PAIR, sems.at[k])
            for copy in more:
                copy.start()
            copies += more
    for copy in copies:
        copy.wait()


def on_device(sky, thresholds):
    rows, columns = sky.shape
    row_count, col_count = lax.axis_size("rows"), lax.axis_size("cols")
    blocks, pairs = columns // LANES, columns // PAIR
    first = blocks // 2 + 2
    weights = [
        [jnp.asarray(w if k else np.concatenate([w, w])) for k, w in enumerate(column_weights(scale + 1))]
        for scale in range(SCALES)
    ]

    in_vmem = pl.BlockSpec(memory_space=pltpu.VMEM)
    in_smem = pl.BlockSpec(memory_space=pltpu.SMEM)
    any_space = pl.BlockSpec(memory_space=pl.ANY)
    in_hbm = pl.BlockSpec(memory_space=pltpu.HBM)
    dma = pltpu.SemaphoreType.DMA

    def room(mebibytes):
        return pltpu.CompilerParams(vmem_limit_bytes=mebibytes * MEBI)

    def array(width):
        return jax.ShapeDtypeStruct((rows, width), F32)

    def vmem(width):
        return pltpu.VMEM((rows, width), F32)

    def operand(slots):
        return pltpu.VMEM((slots * rows, 2 * SPAN), BF16)

    def even_swap(values):
        return lax.ppermute(values, "rows", swaps(row_count, 0))

    def odd_swap(values):
        return lax.ppermute(values, "rows", swaps(row_count, 1))

    def exchange(values):
        return even_swap(values), odd_swap(values)

    widths = (first * LANES, (blocks - first + 1) * LANES)
    part, one, two = pl.pallas_call(
        take_kernel,
        out_shape=(array(widths[0]), array(LANES), array(LANES)),
        in_specs=[in_vmem],
        out_specs=(in_vmem,) * 3,
        compiler_params=room(8),
        name="take",
    )(sky)
    near = [exchange(part)]
    one = lax.ppermute(one, "cols", swaps(col_count, 0))
    two = lax.ppermute(two, "cols", swaps(col_count, 1))
    rest = pl.pallas_call(
        join_kernel,
        out_shape=array(widths[1]),
        in_specs=[in_vmem] * 3,
        out_specs=in_vmem,
        compiler_params=room(8),
        cost_estimate=pl.CostEstimate(flops=3 * 10**10, bytes_accessed=10**6, transcendentals=0),
        name="join",
    )(sky, one, two)
    near.append(exchange(rest))
    beyond = [odd_swap(even) for even, _ in near]
    own = (part, rest)
    group = 8

    row_buffers = [pltpu.VMEM((3 * rows - cut, LANES), F32) for _ in range(group) for cut in (0, 8, 16)]

    def smooth_rows(which, name):
        width = widths[which]
        return pl.pallas_call(
            functools.partial(rows_kernel, group),
            out_shape=array(width),
            in_specs=[in_vmem] * 3,
            out_specs=in_vmem,
            scratch_shapes=[vmem(width)] + row_buffers,
            compiler_params=room(10),
            name=name,
        )(own[which], *near[which])

    four = [smooth_rows(0, "rows_one"), smooth_rows(1, "rows_two")]
    even_four = [even_swap(values) for values in four]

    def columnwise(pairs_of_inputs):
        return [x[0] for x in pairs_of_inputs] + [x[1] for x in pairs_of_inputs]

    fine = [w for scale in range(4) for w in weights[scale]]
    part_sum, plane = pl.pallas_call(
        functools.partial(details_kernel, pairs, tuple(len(weights[scale]) for scale in range(4))),
        out_shape=(array(columns), array(columns)),
        in_specs=[in_smem] + [in_vmem] * (8 + len(fine)),
        out_specs=(in_vmem, in_vmem),
        scratch_shapes=[vmem(w) for w in widths]
        + [operand(pairs + 2)] * 4
        + [pltpu.VMEM((n, LANES), F32) for _ in range(2) for n in (3 * rows, rows + 24, rows + 16)],
        compiler_params=room(28),
        name="details",
    )(thresholds, *own, *columnwise(near), *four, *fine)

    def smooth_far(which, name, *after):
        return pl.pallas_call(
            functools.partial(far_kernel, group, len(after)),
            out_shape=array(widths[which]),
            in_specs=[in_vmem] * 3 + [any_space] * len(after),
            out_specs=in_vmem,
            scratch_shapes=row_buffers,
            compiler_params=room(10),
            name=name,
        )(near[which][1], own[which], beyond[which], *after)

    inner = first // 2 - 2
    far_one = smooth_far(0, "far_one")
    outs = pl.pallas_call(
        coarse_one_kernel,
        out_shape=(array(inner * PAIR),) * 2,
        in_specs=[in_smem] + [in_vmem] * 7,
        out_specs=(in_vmem,) * 2,
        scratch_shapes=[vmem(widths[0]), operand(inner + 2)],
        compiler_params=room(16),
        name="coarse_one",
    )(thresholds, four[0], even_four[0], far_one, part_sum, plane, *weights[4])
    count = pairs - inner
    far_two = smooth_far(1, "far_two", outs[0])
    return pl.pallas_call(
        coarse_two_kernel,
        out_shape=(array(columns), array(columns)),
        in_specs=[in_smem] + [in_vmem] * 12,
        out_specs=(in_hbm,) * 2,
        scratch_shapes=[vmem(w) for w in widths]
        + [operand(count + 2)]
        + [vmem(n * PAIR) for n in (count // 2, count // 2, count - count // 2, count - count // 2)]
        + [dma((8, rows // TILE))],
        compiler_params=room(16),
        name="coarse_two",
    )(thresholds, *four, *even_four, far_one, far_two, part_sum, plane, *weights[4], *outs)


def solution(mesh):
    return jax.shard_map(
        on_device,
        mesh=mesh,
        in_specs=(P("rows", "cols"), P()),
        out_specs=(P("rows", "cols"), P("rows", "cols")),
        check_vma=False,
    )
```

```python
import functools

import jax
import jax.numpy as jnp
import ml_dtypes
import numpy as np
from jax import lax
from jax.experimental import pallas as pl
from jax.experimental.pallas import tpu as pltpu
from jax.sharding import PartitionSpec as P

LANES = 128
HALF = LANES // 2
PAIR = 2 * LANES
SPAN = PAIR + LANES
TILE = 8
SCALES = 5
MEBI = 1024 * 1024
BATCH = 16
STEPS = 4
F32, BF16 = jnp.float32, jnp.bfloat16


def swaps(count, first):
    return [(i, j) for k in range(first, count - 1, 2) for i, j in ((k, k + 1), (k + 1, k))]


def column_weights(scales):
    taps = np.ones(1)
    for scale in range(scales):
        step = np.zeros(4 * 2**scale + 1)
        step[:: 2**scale] = (1.0, 4.0, 6.0, 4.0, 1.0)
        taps = np.convolve(taps, step)
    reach = len(taps) // 2
    source = np.concatenate([np.arange(PAIR + HALF), np.arange(-HALF, 0)])
    offset = source[:, None] - np.arange(PAIR)[None, :]
    exact = np.where(np.abs(offset) <= reach, taps[np.clip(offset + reach, 0, 2 * reach)], 0.0) * 2.0 ** (-8 * scales)
    high = exact.astype(ml_dtypes.bfloat16)
    low = (exact - high.astype(np.float64)).astype(ml_dtypes.bfloat16)
    return [high, low] if np.any(low.astype(np.float32)) else [high]


def binomial(a, b, c, d, e):
    return (a + e) + 4.0 * (b + d) + 6.0 * c


def columns_of(block, width=LANES):
    if isinstance(block, int):
        return slice(block * width, (block + 1) * width)
    return pl.ds(pl.multiple_of(block * width, width), width)


def loop(begin, end, body, group=1):
    def step(k, carry):
        for slot in range(group):
            body(begin + k * group + slot, slot)
        return carry

    whole = (end - begin) // group
    lax.fori_loop(0, whole, step, 0)
    for index in range(begin + whole * group, end):
        body(index, index - begin - whole * group)


def with_neighbours(own, odd_in, flipped, run, prepare=None):
    rows = own[0].shape[0]
    index, last = lax.axis_index("rows"), lax.axis_size("rows") - 1
    outer = jnp.logical_or(index == 0, index == last)

    @pl.when(outer)
    def _():
        for source, target in zip(own, flipped):
            for k in range(rows):
                target[k : k + 1, :] = source[rows - 1 - k : rows - k, :]
        run(flipped)

    @pl.when(jnp.logical_not(outer))
    def _():
        if prepare is not None:
            prepare()
        run(odd_in)


def load_block(own, even, odd, buffer):
    rows = own.shape[0]
    parity = lax.axis_index("rows") % 2
    buffer[rows : 2 * rows, :] = own
    buffer[pl.ds(pl.multiple_of((1 - parity) * 2 * rows, TILE), rows), :] = even
    buffer[pl.ds(pl.multiple_of(parity * 2 * rows, TILE), rows), :] = odd


def taps(buffer, begin, step, count):
    return [buffer[begin + k * step : begin + k * step + count, :] for k in (-2, -1, 0, 1, 2)]


def take_kernel(sky, part, first, second):
    columns = sky.shape[1]
    part[...] = sky[:, 0 : part.shape[1]]
    left, right = sky[:, 0:LANES], sky[:, columns - LANES : columns]
    even = lax.axis_index("cols") % 2 == 0
    first[...] = jnp.where(even, right, left)
    second[...] = jnp.where(even, left, right)


def join_kernel(sky, first, second, rest):
    width, columns = rest.shape[1] - LANES, sky.shape[1]
    rest[:, 0:width] = sky[:, columns - width : columns]
    rows = sky.shape[0]
    index, last = lax.axis_index("cols"), lax.axis_size("cols") - 1
    in_first = lax.broadcasted_iota(jnp.int32, (rows, LANES), 1) < HALF
    even = index % 2 == 0
    left = jnp.where(even, second[...], first[...])
    right = jnp.where(even, first[...], second[...])
    halo = slice(width, width + LANES)
    rest[:, halo] = jnp.where(in_first, right, left)

    def flip(value):
        row = lax.broadcasted_iota(jnp.int32, (LANES, LANES), 0)
        lane = lax.broadcasted_iota(jnp.int32, (LANES, LANES), 1)
        turn = (row + lane == LANES - 1).astype(F32)
        return jnp.dot(value, turn, preferred_element_type=F32, precision=lax.Precision.HIGHEST)

    @pl.when(index == 0)
    def _():
        rest[:, halo] = jnp.where(in_first, right, flip(sky[:, 0:LANES]))

    @pl.when(index == last)
    def _():
        rest[:, halo] = jnp.where(in_first, flip(sky[:, columns - LANES : columns]), left)


def smooth_tile(group, own, even_in, odd_in, out, buffers):
    rows = own.shape[0]

    def one(block, slot):
        zero, ones, twos = buffers[3 * slot : 3 * slot + 3]
        columns = columns_of(block)
        load_block(own[:, columns], even_in[:, columns], odd_in[:, columns], zero)
        ones[...] = binomial(*taps(zero, 4, 1, 3 * rows - 8))
        two = binomial(*taps(ones, 4, 2, 3 * rows - 16))
        twos[...] = two
        n = 3 * rows - 32
        three = binomial(two[0:n], twos[4 : n + 4, :], two[8 : n + 8], twos[12 : n + 12, :], two[16 : n + 16])
        out[:, columns] = binomial(*[three[8 * k : 8 * k + rows] for k in range(5)])

    loop(0, own.shape[1] // LANES, one, group)


def rows_kernel(group, own, even_in, odd_in, out, flipped, *buffers):
    def run(odd):
        smooth_tile(group, own, even_in, odd[0], out, buffers)

    with_neighbours((own,), (odd_in,), (flipped,), run)


def far_kernel(group, after, own, even_in, odd_in, *refs):
    out, *buffers = refs[after:]
    smooth_tile(group, own, even_in, odd_in, out, buffers)


def put(value, operand, rows, main=None, after=None, before=None):
    high = value.astype(BF16)
    low = (value - high.astype(F32)).astype(BF16)

    def at(slot):
        return slice(slot * rows, (slot + 1) * rows) if isinstance(slot, int) else pl.ds(pl.multiple_of(slot * rows, 16), rows)

    for base, piece in ((0, high), (SPAN, low)):
        if main is not None:
            operand[at(main[0]), base + main[1] * LANES : base + (main[1] + 1) * LANES] = piece
        if after is not None:
            operand[at(after), base + PAIR : base + PAIR + HALF] = piece[:, :HALF]
        if before is not None:
            operand[at(before), base + PAIR + HALF : base + SPAN] = piece[:, HALF:]


def clip(detail, level):
    return jnp.minimum(jnp.maximum(detail, -level), level)


def filter_columns(operand, weights, rows, start, count, emit):
    value = operand[start * rows : (start + count) * rows, :]
    total = None
    for weight in weights:
        term = jnp.dot(value[:, : weight.shape[0]], weight[...], preferred_element_type=F32)
        total = term if total is None else total + term
    for k in range(count):
        emit(start + k, total[k * rows : (k + 1) * rows])


def details_kernel(pairs, weight_counts, levels, *refs):
    own, even_in, odd_in, four, refs = refs[:2], refs[2:4], refs[4:6], refs[6:8], refs[8:]
    weights, refs = refs[: sum(weight_counts)], refs[sum(weight_counts) :]
    out, plane, refs = refs[0], refs[1], refs[2:]
    flipped, operands, buffers = refs[:2], refs[2:6], refs[6:]
    rows = own[0].shape[0]
    first = own[0].shape[1] // PAIR

    def keep(odd):
        for source, target in zip(odd, flipped):
            if source is not target:
                target[...] = source[...]

    with_neighbours(own, odd_in, flipped, keep)

    def one(span, block, slot):
        zero, ones, twos = buffers[3 * slot : 3 * slot + 3]
        columns = columns_of(block)
        load_block(own[span][:, columns], even_in[span][:, columns], flipped[span][:, columns], zero)
        ones[...] = binomial(*taps(zero, rows - 12, 1, rows + 24))
        two = binomial(*taps(ones, 4, 2, rows + 16))
        twos[...] = two
        three = binomial(two[0:rows], twos[4 : rows + 4, :], two[8 : rows + 8], twos[12 : rows + 12, :], two[16 : rows + 16])
        return ones[12 : rows + 12, :], two[8 : rows + 8], three, four[span][:, columns]

    def one_pair(span, begin, pair, slot):
        block = 2 * (pair - begin)
        left, right = one(span, block, 2 * slot), one(span, block + 1, 2 * slot + 1)
        for k in range(4):
            put(left[k], operands[k], rows, main=(pair + 1, 0), after=pair)
            put(right[k], operands[k], rows, main=(pair + 1, 1), before=pair + 2)

    for k, value in enumerate(one(1, 2 * (pairs - first), 0)):
        put(value, operands[k], rows, after=pairs, before=1)
    loop(0, first, lambda pair, slot: one_pair(0, 0, pair, slot), 2)
    def columns_step(scale, start, count):
        def emit(slot, total):
            pair = slot - 1
            columns = columns_of(pair, PAIR)
            if scale == 0:
                sky = own[0][:, columns] if pair < first else own[1][:, columns_of(pair - first, PAIR)]
                out[:, columns] = sky - clip(sky - total, levels[scale : scale + 1, :])
            else:
                out[:, columns] = out[:, columns] - clip(plane[:, columns] - total, levels[scale : scale + 1, :])
            plane[:, columns] = total

        use = weights[sum(weight_counts[:scale]) : sum(weight_counts[: scale + 1])]
        filter_columns(operands[scale], use, rows, start + 1, count, emit)

    waiting = list(range(first, pairs))
    share = -(-len(waiting) // STEPS)
    for scale in range(4):
        for start in range(0, first - 1, BATCH):
            count = min(BATCH, first - 1 - start)
            columns_step(scale, start, count)
            for pair in waiting[:share]:
                one_pair(1, first, pair, pair % 4)
            waiting = waiting[share:]
    for pair in waiting:
        one_pair(1, first, pair, pair % 4)
    for scale in range(4):
        columns_step(scale, first - 1, pairs - first + 1)


def last_rows(own, even_in, odd, then):
    half = own[0].shape[0] // 2

    def with_sides(above, below):
        def one(span, block):
            columns = columns_of(block)
            a, b = above[span][0:half, columns], above[span][half : 2 * half, columns]
            c, d = own[span][0:half, columns], own[span][half : 2 * half, columns]
            e, f = below[span][0:half, columns], below[span][half : 2 * half, columns]
            return jnp.concatenate([binomial(a, b, c, d, e), binomial(b, c, d, e, f)], axis=0)

        then(one)

    parity = lax.axis_index("rows") % 2
    pl.when(parity == 0)(lambda: with_sides(odd, even_in))
    pl.when(parity == 1)(lambda: with_sides(even_in, odd))


def finish(operand, weights, rows, start, count, level, pair_of, part_sum, plane, denoised, coarse):
    def emit(slot, total):
        columns, place = columns_of(pair_of(slot), PAIR), columns_of(slot - start, PAIR)
        coarse[:, place] = total
        denoised[:, place] = part_sum[:, columns] - clip(plane[:, columns] - total, level)

    filter_columns(operand, weights, rows, start, count, emit)


def row_copies(source, target, begin, sems):
    columns = slice(begin, begin + source.shape[1])
    return [
        pltpu.make_async_copy(source.at[row : row + TILE, :], target.at[row : row + TILE, columns], sems.at[k])
        for k, row in enumerate(range(0, source.shape[0], TILE))
    ]


def coarse_one_kernel(levels, own, even_in, odd_in, part_sum, plane, high, low, denoised, coarse, flipped, operand):
    rows = own.shape[0]
    pairs = own.shape[1] // PAIR

    def blocks(one):
        def body(pair, _):
            put(one(0, 2 * pair), operand, rows, main=(pair, 0), after=pair - 1)
            put(one(0, 2 * pair + 1), operand, rows, main=(pair, 1), before=pair + 1)

        put(one(0, 1), operand, rows, before=1)
        loop(1, pairs - 1, body)
        put(one(0, 2 * pairs - 2), operand, rows, after=pairs - 2)

    with_neighbours((own,), (odd_in,), (flipped,), lambda odd: last_rows((own,), (even_in,), odd, blocks))
    finish(operand, (high, low), rows, 1, pairs - 2, levels[4:5, :], lambda slot: slot, part_sum, plane, denoised, coarse)


def coarse_two_kernel(levels, *refs):
    own, even_in, refs = refs[:2], refs[2:4], refs[4:]
    far, part_sum, plane, high, low, den_one, coa_one, denoised, coarse, *refs = refs[:2], *refs[2:]
    flipped, (operand, den_two, coa_two, den_three, coa_three, sems) = refs[:2], refs[2:]
    rows, columns = part_sum.shape
    first, pairs = own[0].shape[1] // PAIR, columns // PAIR
    begin = first - 1
    copies = row_copies(den_one, denoised, PAIR, sems.at[6]) + row_copies(coa_one, coarse, PAIR, sems.at[7])
    for copy in copies:
        copy.start()

    def blocks(one):
        def body(pair, _):
            block = 2 * (pair - first)
            put(one(1, block), operand, rows, main=(pair - begin + 1, 0), after=pair - begin)
            put(one(1, block + 1), operand, rows, main=(pair - begin + 1, 1), before=pair - begin + 2)

        loop(first, pairs, body)
        put(one(0, 2 * begin), operand, rows, main=(1, 0))
        put(one(0, 2 * begin + 1), operand, rows, main=(1, 1), before=2)
        put(one(0, 2 * begin - 1), operand, rows, before=1)
        put(one(1, 2 * (pairs - first)), operand, rows, after=pairs - begin, before=0)
        put(one(0, 0), operand, rows, main=(0, 0))
        put(one(0, 1), operand, rows, main=(0, 1))
        put(one(0, 2), operand, rows, after=0)

    with_neighbours(own, far, flipped, lambda odd: last_rows(own, even_in, odd, blocks))
    count = pairs - begin + 1
    half = count // 2
    pair_of = lambda slot: slot + begin - 1 if slot else 0
    for start, size, den, coa, at in ((0, half, den_two, coa_two, 0), (half, count - half, den_three, coa_three, 4)):
        finish(operand, (high, low), rows, start, size, levels[4:5, :], pair_of, part_sum, plane, den, coa)
        for source, target, k in ((den, denoised, at), (coa, coarse, at + 1)):
            if start == 0:
                more = row_copies(source.at[:, 0:PAIR], target, 0, sems.at[k])
                more += row_copies(source.at[:, PAIR : half * PAIR], target, begin * PAIR, sems.at[k + 2])
            else:
                more = row_copies(source, target, (begin + half - 1) * PAIR, sems.at[k])
            for copy in more:
                copy.start()
            copies += more
    for copy in copies:
        copy.wait()


def on_device(sky, thresholds):
    rows, columns = sky.shape
    row_count, col_count = lax.axis_size("rows"), lax.axis_size("cols")
    blocks, pairs = columns // LANES, columns // PAIR
    first = blocks // 2 + 2
    weights = [
        [jnp.asarray(w if k else np.concatenate([w, w])) for k, w in enumerate(column_weights(scale + 1))]
        for scale in range(SCALES)
    ]

    in_vmem = pl.BlockSpec(memory_space=pltpu.VMEM)
    any_space = pl.BlockSpec(memory_space=pl.ANY)
    in_hbm = pl.BlockSpec(memory_space=pltpu.HBM)
    dma = pltpu.SemaphoreType.DMA

    def room(mebibytes):
        return pltpu.CompilerParams(vmem_limit_bytes=mebibytes * MEBI)

    def array(width):
        return jax.ShapeDtypeStruct((rows, width), F32)

    def vmem(width):
        return pltpu.VMEM((rows, width), F32)

    def operand(slots):
        return pltpu.VMEM((slots * rows, 2 * SPAN), BF16)

    def even_swap(values):
        return lax.ppermute(values, "rows", swaps(row_count, 0))

    def odd_swap(values):
        return lax.ppermute(values, "rows", swaps(row_count, 1))

    def exchange(values):
        return even_swap(values), odd_swap(values)

    levels = jnp.broadcast_to(thresholds[:, None], (SCALES, PAIR))
    widths = (first * LANES, (blocks - first + 1) * LANES)
    part, one, two = pl.pallas_call(
        take_kernel,
        out_shape=(array(widths[0]), array(LANES), array(LANES)),
        in_specs=[in_vmem],
        out_specs=(in_vmem,) * 3,
        compiler_params=room(8),
        name="take",
    )(sky)
    near = [exchange(part)]
    one = lax.ppermute(one, "cols", swaps(col_count, 0))
    two = lax.ppermute(two, "cols", swaps(col_count, 1))
    rest = pl.pallas_call(
        join_kernel,
        out_shape=array(widths[1]),
        in_specs=[in_vmem] * 3,
        out_specs=in_vmem,
        compiler_params=room(8),
        cost_estimate=pl.CostEstimate(flops=3 * 10**10, bytes_accessed=10**6, transcendentals=0),
        name="join",
    )(sky, one, two)
    near.append(exchange(rest))
    beyond = [odd_swap(even) for even, _ in near]
    own = (part, rest)
    group = 8

    row_buffers = [pltpu.VMEM((3 * rows - cut, LANES), F32) for _ in range(group) for cut in (0, 8, 16)]

    def smooth_rows(which, name):
        width = widths[which]
        return pl.pallas_call(
            functools.partial(rows_kernel, group),
            out_shape=array(width),
            in_specs=[in_vmem] * 3,
            out_specs=in_vmem,
            scratch_shapes=[vmem(width)] + row_buffers,
            compiler_params=room(10),
            name=name,
        )(own[which], *near[which])

    four = [smooth_rows(0, "rows_one"), smooth_rows(1, "rows_two")]
    even_four = [even_swap(values) for values in four]

    def columnwise(pairs_of_inputs):
        return [x[0] for x in pairs_of_inputs] + [x[1] for x in pairs_of_inputs]

    fine = [w for scale in range(4) for w in weights[scale]]
    part_sum, plane = pl.pallas_call(
        functools.partial(details_kernel, pairs, tuple(len(weights[scale]) for scale in range(4))),
        out_shape=(array(columns), array(columns)),
        in_specs=[in_vmem] * (9 + len(fine)),
        out_specs=(in_vmem, in_vmem),
        scratch_shapes=[vmem(w) for w in widths]
        + [operand(pairs + 2)] * 4
        + [pltpu.VMEM((n, LANES), F32) for _ in range(8) for n in (3 * rows, rows + 24, rows + 16)],
        compiler_params=room(28),
        name="details",
    )(levels, *own, *columnwise(near), *four, *fine)

    def smooth_far(which, name, *after):
        return pl.pallas_call(
            functools.partial(far_kernel, group, len(after)),
            out_shape=array(widths[which]),
            in_specs=[in_vmem] * 3 + [any_space] * len(after),
            out_specs=in_vmem,
            scratch_shapes=row_buffers,
            compiler_params=room(10),
            name=name,
        )(near[which][1], own[which], beyond[which], *after)

    inner = first // 2 - 2
    far_one = smooth_far(0, "far_one")
    outs = pl.pallas_call(
        coarse_one_kernel,
        out_shape=(array(inner * PAIR),) * 2,
        in_specs=[in_vmem] * 8,
        out_specs=(in_vmem,) * 2,
        scratch_shapes=[vmem(widths[0]), operand(inner + 2)],
        compiler_params=room(16),
        name="coarse_one",
    )(levels, four[0], even_four[0], far_one, part_sum, plane, *weights[4])
    count = pairs - inner
    far_two = smooth_far(1, "far_two", outs[0])
    return pl.pallas_call(
        coarse_two_kernel,
        out_shape=(array(columns), array(columns)),
        in_specs=[in_vmem] * 13,
        out_specs=(in_hbm,) * 2,
        scratch_shapes=[vmem(w) for w in widths]
        + [operand(count + 2)]
        + [vmem(n * PAIR) for n in (count // 2, count // 2, count - count // 2, count - count // 2)]
        + [dma((8, rows // TILE))],
        compiler_params=room(16),
        name="coarse_two",
    )(levels, *four, *even_four, far_one, far_two, part_sum, plane, *weights[4], *outs)


def solution(mesh):
    return jax.shard_map(
        on_device,
        mesh=mesh,
        in_specs=(P("rows", "cols"), P()),
        out_specs=(P("rows", "cols"), P("rows", "cols")),
        check_vma=False,
    )
```

```python
import functools

import jax
import jax.numpy as jnp
import ml_dtypes
import numpy as np
from jax import lax
from jax.experimental import pallas as pl
from jax.experimental.pallas import tpu as pltpu
from jax.sharding import PartitionSpec as P

LANES = 128
HALF = LANES // 2
PAIR = 2 * LANES
SPAN = PAIR + LANES
TILE = 8
SCALES = 5
MEBI = 1024 * 1024
BATCH = 18
STEPS = 4
F32, BF16 = jnp.float32, jnp.bfloat16


def swaps(count, first):
    return [(i, j) for k in range(first, count - 1, 2) for i, j in ((k, k + 1), (k + 1, k))]


def column_weights(scales):
    taps = np.ones(1)
    for scale in range(scales):
        step = np.zeros(4 * 2**scale + 1)
        step[:: 2**scale] = (1.0, 4.0, 6.0, 4.0, 1.0)
        taps = np.convolve(taps, step)
    reach = len(taps) // 2
    source = np.concatenate([np.arange(PAIR + HALF), np.arange(-HALF, 0)])
    offset = source[:, None] - np.arange(PAIR)[None, :]
    exact = np.where(np.abs(offset) <= reach, taps[np.clip(offset + reach, 0, 2 * reach)], 0.0) * 2.0 ** (-8 * scales)
    high = exact.astype(ml_dtypes.bfloat16)
    low = (exact - high.astype(np.float64)).astype(ml_dtypes.bfloat16)
    return [high, low] if np.any(low.astype(np.float32)) else [high]


def binomial(a, b, c, d, e):
    return (a + e) + 4.0 * (b + d) + 6.0 * c


def columns_of(block, width=LANES):
    if isinstance(block, int):
        return slice(block * width, (block + 1) * width)
    return pl.ds(pl.multiple_of(block * width, width), width)


def loop(begin, end, body, group=1):
    def step(k, carry):
        for slot in range(group):
            body(begin + k * group + slot, slot)
        return carry

    whole = (end - begin) // group
    lax.fori_loop(0, whole, step, 0)
    for index in range(begin + whole * group, end):
        body(index, index - begin - whole * group)


def with_neighbours(own, odd_in, flipped, run, prepare=None):
    rows = own[0].shape[0]
    index, last = lax.axis_index("rows"), lax.axis_size("rows") - 1
    outer = jnp.logical_or(index == 0, index == last)

    @pl.when(outer)
    def _():
        for source, target in zip(own, flipped):
            for k in range(rows):
                target[k : k + 1, :] = source[rows - 1 - k : rows - k, :]
        run(flipped)

    @pl.when(jnp.logical_not(outer))
    def _():
        if prepare is not None:
            prepare()
        run(odd_in)


def load_block(own, even, odd, buffer):
    rows = own.shape[0]
    parity = lax.axis_index("rows") % 2
    buffer[rows : 2 * rows, :] = own
    buffer[pl.ds(pl.multiple_of((1 - parity) * 2 * rows, TILE), rows), :] = even
    buffer[pl.ds(pl.multiple_of(parity * 2 * rows, TILE), rows), :] = odd


def taps(buffer, begin, step, count):
    return [buffer[begin + k * step : begin + k * step + count, :] for k in (-2, -1, 0, 1, 2)]


def take_kernel(sky, part, first, second):
    columns = sky.shape[1]
    part[...] = sky[:, 0 : part.shape[1]]
    left, right = sky[:, 0:LANES], sky[:, columns - LANES : columns]
    even = lax.axis_index("cols") % 2 == 0
    first[...] = jnp.where(even, right, left)
    second[...] = jnp.where(even, left, right)


def join_kernel(sky, first, second, rest):
    width, columns = rest.shape[1] - LANES, sky.shape[1]
    rest[:, 0:width] = sky[:, columns - width : columns]
    rows = sky.shape[0]
    index, last = lax.axis_index("cols"), lax.axis_size("cols") - 1
    in_first = lax.broadcasted_iota(jnp.int32, (rows, LANES), 1) < HALF
    even = index % 2 == 0
    left = jnp.where(even, second[...], first[...])
    right = jnp.where(even, first[...], second[...])
    halo = slice(width, width + LANES)
    rest[:, halo] = jnp.where(in_first, right, left)

    def flip(value):
        row = lax.broadcasted_iota(jnp.int32, (LANES, LANES), 0)
        lane = lax.broadcasted_iota(jnp.int32, (LANES, LANES), 1)
        turn = (row + lane == LANES - 1).astype(F32)
        return jnp.dot(value, turn, preferred_element_type=F32, precision=lax.Precision.HIGHEST)

    @pl.when(index == 0)
    def _():
        rest[:, halo] = jnp.where(in_first, right, flip(sky[:, 0:LANES]))

    @pl.when(index == last)
    def _():
        rest[:, halo] = jnp.where(in_first, flip(sky[:, columns - LANES : columns]), left)


def smooth_tile(group, own, even_in, odd_in, out, buffers):
    rows = own.shape[0]

    def one(block, slot):
        zero, ones, twos = buffers[3 * slot : 3 * slot + 3]
        columns = columns_of(block)
        load_block(own[:, columns], even_in[:, columns], odd_in[:, columns], zero)
        ones[...] = binomial(*taps(zero, 4, 1, 3 * rows - 8))
        two = binomial(*taps(ones, 4, 2, 3 * rows - 16))
        twos[...] = two
        n = 3 * rows - 32
        three = binomial(two[0:n], twos[4 : n + 4, :], two[8 : n + 8], twos[12 : n + 12, :], two[16 : n + 16])
        out[:, columns] = binomial(*[three[8 * k : 8 * k + rows] for k in range(5)])

    loop(0, own.shape[1] // LANES, one, group)


def rows_kernel(group, own, even_in, odd_in, out, flipped, *buffers):
    def run(odd):
        smooth_tile(group, own, even_in, odd[0], out, buffers)

    with_neighbours((own,), (odd_in,), (flipped,), run)


def far_kernel(group, after, own, even_in, odd_in, *refs):
    out, *buffers = refs[after:]
    smooth_tile(group, own, even_in, odd_in, out, buffers)


def put(value, operand, rows, main=None, after=None, before=None):
    high = value.astype(BF16)
    low = (value - high.astype(F32)).astype(BF16)

    def at(slot):
        return slice(slot * rows, (slot + 1) * rows) if isinstance(slot, int) else pl.ds(pl.multiple_of(slot * rows, 16), rows)

    for base, piece in ((0, high), (SPAN, low)):
        if main is not None:
            operand[at(main[0]), base + main[1] * LANES : base + (main[1] + 1) * LANES] = piece
        if after is not None:
            operand[at(after), base + PAIR : base + PAIR + HALF] = piece[:, :HALF]
        if before is not None:
            operand[at(before), base + PAIR + HALF : base + SPAN] = piece[:, HALF:]


def clip(detail, level):
    return jnp.minimum(jnp.maximum(detail, -level), level)


def filter_columns(operand, weights, rows, start, count, emit):
    value = operand[start * rows : (start + count) * rows, :]
    total = None
    for weight in weights:
        term = jnp.dot(value[:, : weight.shape[0]], weight[...], preferred_element_type=F32)
        total = term if total is None else total + term
    for k in range(count):
        emit(start + k, total[k * rows : (k + 1) * rows])


def details_kernel(pairs, weight_counts, levels, *refs):
    own, even_in, odd_in, four, refs = refs[:2], refs[2:4], refs[4:6], refs[6:8], refs[8:]
    weights, refs = refs[: sum(weight_counts)], refs[sum(weight_counts) :]
    out, plane, refs = refs[0], refs[1], refs[2:]
    flipped, operands, buffers = refs[:2], refs[2:6], refs[6:]
    rows = own[0].shape[0]
    first = own[0].shape[1] // PAIR

    def keep(odd):
        for source, target in zip(odd, flipped):
            if source is not target:
                target[...] = source[...]

    with_neighbours(own, odd_in, flipped, keep)

    def one(span, block, slot):
        zero, ones, twos = buffers[3 * slot : 3 * slot + 3]
        columns = columns_of(block)
        load_block(own[span][:, columns], even_in[span][:, columns], flipped[span][:, columns], zero)
        ones[...] = binomial(*taps(zero, rows - 12, 1, rows + 24))
        two = binomial(*taps(ones, 4, 2, rows + 16))
        twos[...] = two
        three = binomial(two[0:rows], twos[4 : rows + 4, :], two[8 : rows + 8], twos[12 : rows + 12, :], two[16 : rows + 16])
        return ones[12 : rows + 12, :], two[8 : rows + 8], three, four[span][:, columns]

    def one_pair(span, begin, pair, slot):
        block = 2 * (pair - begin)
        left, right = one(span, block, 2 * slot), one(span, block + 1, 2 * slot + 1)
        for k in range(4):
            put(left[k], operands[k], rows, main=(pair + 1, 0), after=pair)
            put(right[k], operands[k], rows, main=(pair + 1, 1), before=pair + 2)

    for k, value in enumerate(one(1, 2 * (pairs - first), 0)):
        put(value, operands[k], rows, after=pairs, before=1)
    loop(0, first, lambda pair, slot: one_pair(0, 0, pair, slot), 2)
    def columns_step(scale, start, count):
        def emit(slot, total):
            pair = slot - 1
            columns = columns_of(pair, PAIR)
            if scale == 0:
                sky = own[0][:, columns] if pair < first else own[1][:, columns_of(pair - first, PAIR)]
                out[:, columns] = sky - clip(sky - total, levels[scale : scale + 1, :])
            else:
                out[:, columns] = out[:, columns] - clip(plane[:, columns] - total, levels[scale : scale + 1, :])
            plane[:, columns] = total

        use = weights[sum(weight_counts[:scale]) : sum(weight_counts[: scale + 1])]
        filter_columns(operands[scale], use, rows, start + 1, count, emit)

    waiting = list(range(first, pairs))
    share = -(-len(waiting) // STEPS)
    for scale in range(4):
        for start in range(0, first - 1, BATCH):
            count = min(BATCH, first - 1 - start)
            columns_step(scale, start, count)
            for pair in waiting[:share]:
                one_pair(1, first, pair, pair % 4)
            waiting = waiting[share:]
    for pair in waiting:
        one_pair(1, first, pair, pair % 4)
    for scale in range(4):
        columns_step(scale, first - 1, pairs - first + 1)


def last_rows(own, even_in, odd, then):
    half = own[0].shape[0] // 2

    def with_sides(above, below):
        def one(span, block):
            columns = columns_of(block)
            a, b = above[span][0:half, columns], above[span][half : 2 * half, columns]
            c, d = own[span][0:half, columns], own[span][half : 2 * half, columns]
            e, f = below[span][0:half, columns], below[span][half : 2 * half, columns]
            return jnp.concatenate([binomial(a, b, c, d, e), binomial(b, c, d, e, f)], axis=0)

        then(one)

    parity = lax.axis_index("rows") % 2
    pl.when(parity == 0)(lambda: with_sides(odd, even_in))
    pl.when(parity == 1)(lambda: with_sides(even_in, odd))


def finish(operand, weights, rows, start, count, level, pair_of, part_sum, plane, denoised, coarse):
    def emit(slot, total):
        columns, place = columns_of(pair_of(slot), PAIR), columns_of(slot - start, PAIR)
        coarse[:, place] = total
        denoised[:, place] = part_sum[:, columns] - clip(plane[:, columns] - total, level)

    filter_columns(operand, weights, rows, start, count, emit)


def row_copies(source, target, begin, sems):
    columns = slice(begin, begin + source.shape[1])
    return [
        pltpu.make_async_copy(source.at[row : row + TILE, :], target.at[row : row + TILE, columns], sems.at[k])
        for k, row in enumerate(range(0, source.shape[0], TILE))
    ]


def coarse_one_kernel(levels, own, even_in, odd_in, part_sum, plane, high, low, denoised, coarse, flipped, operand):
    rows = own.shape[0]
    pairs = own.shape[1] // PAIR

    def blocks(one):
        def body(pair, _):
            put(one(0, 2 * pair), operand, rows, main=(pair, 0), after=pair - 1)
            put(one(0, 2 * pair + 1), operand, rows, main=(pair, 1), before=pair + 1)

        put(one(0, 1), operand, rows, before=1)
        loop(1, pairs - 1, body)
        put(one(0, 2 * pairs - 2), operand, rows, after=pairs - 2)

    with_neighbours((own,), (odd_in,), (flipped,), lambda odd: last_rows((own,), (even_in,), odd, blocks))
    finish(operand, (high, low), rows, 1, pairs - 2, levels[4:5, :], lambda slot: slot, part_sum, plane, denoised, coarse)


def coarse_two_kernel(levels, *refs):
    own, even_in, refs = refs[:2], refs[2:4], refs[4:]
    far, part_sum, plane, high, low, den_one, coa_one, denoised, coarse, *refs = refs[:2], *refs[2:]
    flipped, (operand, den_two, coa_two, den_three, coa_three, sems) = refs[:2], refs[2:]
    rows, columns = part_sum.shape
    first, pairs = own[0].shape[1] // PAIR, columns // PAIR
    begin = first - 1
    copies = row_copies(den_one, denoised, PAIR, sems.at[6]) + row_copies(coa_one, coarse, PAIR, sems.at[7])
    for copy in copies:
        copy.start()

    def blocks(one):
        def body(pair, _):
            block = 2 * (pair - first)
            put(one(1, block), operand, rows, main=(pair - begin + 1, 0), after=pair - begin)
            put(one(1, block + 1), operand, rows, main=(pair - begin + 1, 1), before=pair - begin + 2)

        loop(first, pairs, body)
        put(one(0, 2 * begin), operand, rows, main=(1, 0))
        put(one(0, 2 * begin + 1), operand, rows, main=(1, 1), before=2)
        put(one(0, 2 * begin - 1), operand, rows, before=1)
        put(one(1, 2 * (pairs - first)), operand, rows, after=pairs - begin, before=0)
        put(one(0, 0), operand, rows, main=(0, 0))
        put(one(0, 1), operand, rows, main=(0, 1))
        put(one(0, 2), operand, rows, after=0)

    with_neighbours(own, far, flipped, lambda odd: last_rows(own, even_in, odd, blocks))
    count = pairs - begin + 1
    half = count // 2
    pair_of = lambda slot: slot + begin - 1 if slot else 0
    for start, size, den, coa, at in ((0, half, den_two, coa_two, 0), (half, count - half, den_three, coa_three, 4)):
        finish(operand, (high, low), rows, start, size, levels[4:5, :], pair_of, part_sum, plane, den, coa)
        for source, target, k in ((den, denoised, at), (coa, coarse, at + 1)):
            if start == 0:
                more = row_copies(source.at[:, 0:PAIR], target, 0, sems.at[k])
                more += row_copies(source.at[:, PAIR : half * PAIR], target, begin * PAIR, sems.at[k + 2])
            else:
                more = row_copies(source, target, (begin + half - 1) * PAIR, sems.at[k])
            for copy in more:
                copy.start()
            copies += more
    for copy in copies:
        copy.wait()


def on_device(sky, thresholds):
    rows, columns = sky.shape
    row_count, col_count = lax.axis_size("rows"), lax.axis_size("cols")
    blocks, pairs = columns // LANES, columns // PAIR
    first = blocks // 2 + 6
    weights = [
        [jnp.asarray(w if k else np.concatenate([w, w])) for k, w in enumerate(column_weights(scale + 1))]
        for scale in range(SCALES)
    ]

    in_vmem = pl.BlockSpec(memory_space=pltpu.VMEM)
    any_space = pl.BlockSpec(memory_space=pl.ANY)
    in_hbm = pl.BlockSpec(memory_space=pltpu.HBM)
    dma = pltpu.SemaphoreType.DMA

    def room(mebibytes):
        return pltpu.CompilerParams(vmem_limit_bytes=mebibytes * MEBI)

    def array(width):
        return jax.ShapeDtypeStruct((rows, width), F32)

    def vmem(width):
        return pltpu.VMEM((rows, width), F32)

    def operand(slots):
        return pltpu.VMEM((slots * rows, 2 * SPAN), BF16)

    def even_swap(values):
        return lax.ppermute(values, "rows", swaps(row_count, 0))

    def odd_swap(values):
        return lax.ppermute(values, "rows", swaps(row_count, 1))

    def exchange(values):
        return even_swap(values), odd_swap(values)

    levels = jnp.broadcast_to(thresholds[:, None], (SCALES, PAIR))
    widths = (first * LANES, (blocks - first + 1) * LANES)
    part, one, two = pl.pallas_call(
        take_kernel,
        out_shape=(array(widths[0]), array(LANES), array(LANES)),
        in_specs=[in_vmem],
        out_specs=(in_vmem,) * 3,
        compiler_params=room(8),
        name="take",
    )(sky)
    near = [exchange(part)]
    one = lax.ppermute(one, "cols", swaps(col_count, 0))
    two = lax.ppermute(two, "cols", swaps(col_count, 1))
    rest = pl.pallas_call(
        join_kernel,
        out_shape=array(widths[1]),
        in_specs=[in_vmem] * 3,
        out_specs=in_vmem,
        compiler_params=room(8),
        cost_estimate=pl.CostEstimate(flops=3 * 10**10, bytes_accessed=10**6, transcendentals=0),
        name="join",
    )(sky, one, two)
    near.append(exchange(rest))
    beyond = [odd_swap(even) for even, _ in near]
    own = (part, rest)
    group = 8

    row_buffers = [pltpu.VMEM((3 * rows - cut, LANES), F32) for _ in range(group) for cut in (0, 8, 16)]

    def smooth_rows(which, name):
        width = widths[which]
        return pl.pallas_call(
            functools.partial(rows_kernel, group),
            out_shape=array(width),
            in_specs=[in_vmem] * 3,
            out_specs=in_vmem,
            scratch_shapes=[vmem(width)] + row_buffers,
            compiler_params=room(10),
            name=name,
        )(own[which], *near[which])

    four = [smooth_rows(0, "rows_one"), smooth_rows(1, "rows_two")]
    even_four = [even_swap(values) for values in four]

    def columnwise(pairs_of_inputs):
        return [x[0] for x in pairs_of_inputs] + [x[1] for x in pairs_of_inputs]

    fine = [w for scale in range(4) for w in weights[scale]]
    part_sum, plane = pl.pallas_call(
        functools.partial(details_kernel, pairs, tuple(len(weights[scale]) for scale in range(4))),
        out_shape=(array(columns), array(columns)),
        in_specs=[in_vmem] * (9 + len(fine)),
        out_specs=(in_vmem, in_vmem),
        scratch_shapes=[vmem(w) for w in widths]
        + [operand(pairs + 2)] * 4
        + [pltpu.VMEM((n, LANES), F32) for _ in range(8) for n in (3 * rows, rows + 24, rows + 16)],
        compiler_params=room(28),
        name="details",
    )(levels, *own, *columnwise(near), *four, *fine)

    def smooth_far(which, name, *after):
        return pl.pallas_call(
            functools.partial(far_kernel, group, len(after)),
            out_shape=array(widths[which]),
            in_specs=[in_vmem] * 3 + [any_space] * len(after),
            out_specs=in_vmem,
            scratch_shapes=row_buffers,
            compiler_params=room(10),
            name=name,
        )(near[which][1], own[which], beyond[which], *after)

    inner = first // 2 - 2
    far_one = smooth_far(0, "far_one")
    outs = pl.pallas_call(
        coarse_one_kernel,
        out_shape=(array(inner * PAIR),) * 2,
        in_specs=[in_vmem] * 8,
        out_specs=(in_vmem,) * 2,
        scratch_shapes=[vmem(widths[0]), operand(inner + 2)],
        compiler_params=room(16),
        name="coarse_one",
    )(levels, four[0], even_four[0], far_one, part_sum, plane, *weights[4])
    count = pairs - inner
    far_two = smooth_far(1, "far_two", outs[0])
    return pl.pallas_call(
        coarse_two_kernel,
        out_shape=(array(columns), array(columns)),
        in_specs=[in_vmem] * 13,
        out_specs=(in_hbm,) * 2,
        scratch_shapes=[vmem(w) for w in widths]
        + [operand(count + 2)]
        + [vmem(n * PAIR) for n in (count // 2, count // 2, count - count // 2, count - count // 2)]
        + [dma((8, rows // TILE))],
        compiler_params=room(16),
        name="coarse_two",
    )(levels, *four, *even_four, far_one, far_two, part_sum, plane, *weights[4], *outs)


def solution(mesh):
    return jax.shard_map(
        on_device,
        mesh=mesh,
        in_specs=(P("rows", "cols"), P()),
        out_specs=(P("rows", "cols"), P("rows", "cols")),
        check_vma=False,
    )
```

```python
import functools

import jax
import jax.numpy as jnp
import ml_dtypes
import numpy as np
from jax import lax
from jax.experimental import pallas as pl
from jax.experimental.pallas import tpu as pltpu
from jax.sharding import PartitionSpec as P

LANES = 128
HALF = LANES // 2
PAIR = 2 * LANES
SPAN = PAIR + LANES
TILE = 8
SCALES = 5
MEBI = 1024 * 1024
BATCH = 18
STEPS = 4
F32, BF16 = jnp.float32, jnp.bfloat16


def swaps(count, first):
    return [(i, j) for k in range(first, count - 1, 2) for i, j in ((k, k + 1), (k + 1, k))]


def column_weights(scales):
    taps = np.ones(1)
    for scale in range(scales):
        step = np.zeros(4 * 2**scale + 1)
        step[:: 2**scale] = (1.0, 4.0, 6.0, 4.0, 1.0)
        taps = np.convolve(taps, step)
    reach = len(taps) // 2
    source = np.concatenate([np.arange(PAIR + HALF), np.arange(-HALF, 0)])
    offset = source[:, None] - np.arange(PAIR)[None, :]
    exact = np.where(np.abs(offset) <= reach, taps[np.clip(offset + reach, 0, 2 * reach)], 0.0) * 2.0 ** (-8 * scales)
    high = exact.astype(ml_dtypes.bfloat16)
    low = (exact - high.astype(np.float64)).astype(ml_dtypes.bfloat16)
    return [high, low] if np.any(low.astype(np.float32)) else [high]


def binomial(a, b, c, d, e):
    return (a + e) + 4.0 * (b + d) + 6.0 * c


def columns_of(block, width=LANES):
    if isinstance(block, int):
        return slice(block * width, (block + 1) * width)
    return pl.ds(pl.multiple_of(block * width, width), width)


def loop(begin, end, body, group=1):
    def step(k, carry):
        for slot in range(group):
            body(begin + k * group + slot, slot)
        return carry

    whole = (end - begin) // group
    lax.fori_loop(0, whole, step, 0)
    for index in range(begin + whole * group, end):
        body(index, index - begin - whole * group)


def with_neighbours(own, odd_in, flipped, run, prepare=None):
    rows = own[0].shape[0]
    index, last = lax.axis_index("rows"), lax.axis_size("rows") - 1
    outer = jnp.logical_or(index == 0, index == last)

    @pl.when(outer)
    def _():
        for source, target in zip(own, flipped):
            for k in range(rows):
                target[k : k + 1, :] = source[rows - 1 - k : rows - k, :]
        run(flipped)

    @pl.when(jnp.logical_not(outer))
    def _():
        if prepare is not None:
            prepare()
        run(odd_in)


def load_block(own, even, odd, buffer):
    rows = own.shape[0]
    parity = lax.axis_index("rows") % 2
    buffer[rows : 2 * rows, :] = own
    buffer[pl.ds(pl.multiple_of((1 - parity) * 2 * rows, TILE), rows), :] = even
    buffer[pl.ds(pl.multiple_of(parity * 2 * rows, TILE), rows), :] = odd


def taps(buffer, begin, step, count):
    return [buffer[begin + k * step : begin + k * step + count, :] for k in (-2, -1, 0, 1, 2)]


def take_kernel(sky, part, first, second):
    columns = sky.shape[1]
    part[...] = sky[:, 0 : part.shape[1]]
    left, right = sky[:, 0:LANES], sky[:, columns - LANES : columns]
    even = lax.axis_index("cols") % 2 == 0
    first[...] = jnp.where(even, right, left)
    second[...] = jnp.where(even, left, right)


def join_kernel(sky, first, second, rest):
    width, columns = rest.shape[1] - LANES, sky.shape[1]
    rest[:, 0:width] = sky[:, columns - width : columns]
    rows = sky.shape[0]
    index, last = lax.axis_index("cols"), lax.axis_size("cols") - 1
    in_first = lax.broadcasted_iota(jnp.int32, (rows, LANES), 1) < HALF
    even = index % 2 == 0
    left = jnp.where(even, second[...], first[...])
    right = jnp.where(even, first[...], second[...])
    halo = slice(width, width + LANES)
    rest[:, halo] = jnp.where(in_first, right, left)

    def flip(value):
        row = lax.broadcasted_iota(jnp.int32, (LANES, LANES), 0)
        lane = lax.broadcasted_iota(jnp.int32, (LANES, LANES), 1)
        turn = (row + lane == LANES - 1).astype(F32)
        return jnp.dot(value, turn, preferred_element_type=F32, precision=lax.Precision.HIGHEST)

    @pl.when(index == 0)
    def _():
        rest[:, halo] = jnp.where(in_first, right, flip(sky[:, 0:LANES]))

    @pl.when(index == last)
    def _():
        rest[:, halo] = jnp.where(in_first, flip(sky[:, columns - LANES : columns]), left)


def smooth_tile(group, own, even_in, odd_in, out, buffers, kept=None):
    rows = own.shape[0]

    def one(block, slot):
        zero, ones, twos = buffers[3 * slot : 3 * slot + 3]
        columns = columns_of(block)
        load_block(own[:, columns], even_in[:, columns], odd_in[:, columns], zero)
        ones[...] = binomial(*taps(zero, 4, 1, 3 * rows - 8))
        two = binomial(*taps(ones, 4, 2, 3 * rows - 16))
        twos[...] = two
        n = 3 * rows - 32
        three = binomial(two[0:n], twos[4 : n + 4, :], two[8 : n + 8], twos[12 : n + 12, :], two[16 : n + 16])
        out[:, columns] = binomial(*[three[8 * k : 8 * k + rows] for k in range(5)])
        if kept is not None:
            kept[0][:, columns] = ones[rows - 4 : 2 * rows - 4, :]
            kept[1][:, columns] = two[rows - 8 : 2 * rows - 8]
            kept[2][:, columns] = three[rows - 16 : 2 * rows - 16]

    loop(0, own.shape[1] // LANES, one, group)


def rows_kernel(group, own, even_in, odd_in, ones, twos, threes, out, flipped, *buffers):
    def run(odd):
        smooth_tile(group, own, even_in, odd[0], out, buffers, (ones, twos, threes))

    with_neighbours((own,), (odd_in,), (flipped,), run)


def far_kernel(group, after, own, even_in, odd_in, *refs):
    out, *buffers = refs[after:]
    smooth_tile(group, own, even_in, odd_in, out, buffers)


def put(value, operand, rows, main=None, after=None, before=None):
    high = value.astype(BF16)
    low = (value - high.astype(F32)).astype(BF16)

    def at(slot):
        return slice(slot * rows, (slot + 1) * rows) if isinstance(slot, int) else pl.ds(pl.multiple_of(slot * rows, 16), rows)

    for base, piece in ((0, high), (SPAN, low)):
        if main is not None:
            operand[at(main[0]), base + main[1] * LANES : base + (main[1] + 1) * LANES] = piece
        if after is not None:
            operand[at(after), base + PAIR : base + PAIR + HALF] = piece[:, :HALF]
        if before is not None:
            operand[at(before), base + PAIR + HALF : base + SPAN] = piece[:, HALF:]


def clip(detail, level):
    return jnp.minimum(jnp.maximum(detail, -level), level)


def filter_columns(operand, weights, rows, start, count, emit):
    value = operand[start * rows : (start + count) * rows, :]
    total = None
    for weight in weights:
        term = jnp.dot(value[:, : weight.shape[0]], weight[...], preferred_element_type=F32)
        total = term if total is None else total + term
    for k in range(count):
        emit(start + k, total[k * rows : (k + 1) * rows])


def details_kernel(pairs, weight_counts, levels, *refs):
    own, smoothed, refs = refs[:2], (refs[2:6], refs[6:10]), refs[10:]
    weights, refs = refs[: sum(weight_counts)], refs[sum(weight_counts) :]
    out, plane, *operands = refs
    rows = own[0].shape[0]
    first = own[0].shape[1] // PAIR

    def one(span, block):
        return [values[:, columns_of(block)] for values in smoothed[span]]

    def one_pair(span, begin, pair):
        block = 2 * (pair - begin)
        left, right = one(span, block), one(span, block + 1)
        for k in range(4):
            put(left[k], operands[k], rows, main=(pair + 1, 0), after=pair)
            put(right[k], operands[k], rows, main=(pair + 1, 1), before=pair + 2)

    for k, value in enumerate(one(1, 2 * (pairs - first))):
        put(value, operands[k], rows, after=pairs, before=1)
    loop(0, first, lambda pair, slot: one_pair(0, 0, pair), 2)
    def columns_step(scale, start, count):
        def emit(slot, total):
            pair = slot - 1
            columns = columns_of(pair, PAIR)
            if scale == 0:
                sky = own[0][:, columns] if pair < first else own[1][:, columns_of(pair - first, PAIR)]
                out[:, columns] = sky - clip(sky - total, levels[scale : scale + 1, :])
            else:
                out[:, columns] = out[:, columns] - clip(plane[:, columns] - total, levels[scale : scale + 1, :])
            plane[:, columns] = total

        use = weights[sum(weight_counts[:scale]) : sum(weight_counts[: scale + 1])]
        filter_columns(operands[scale], use, rows, start + 1, count, emit)

    waiting = list(range(first, pairs))
    share = -(-len(waiting) // STEPS)
    for scale in range(4):
        for start in range(0, first - 1, BATCH):
            count = min(BATCH, first - 1 - start)
            columns_step(scale, start, count)
            for pair in waiting[:share]:
                one_pair(1, first, pair)
            waiting = waiting[share:]
    for pair in waiting:
        one_pair(1, first, pair)
    for scale in range(4):
        columns_step(scale, first - 1, pairs - first + 1)


def last_rows(own, even_in, odd, then):
    half = own[0].shape[0] // 2

    def with_sides(above, below):
        def one(span, block):
            columns = columns_of(block)
            a, b = above[span][0:half, columns], above[span][half : 2 * half, columns]
            c, d = own[span][0:half, columns], own[span][half : 2 * half, columns]
            e, f = below[span][0:half, columns], below[span][half : 2 * half, columns]
            return jnp.concatenate([binomial(a, b, c, d, e), binomial(b, c, d, e, f)], axis=0)

        then(one)

    parity = lax.axis_index("rows") % 2
    pl.when(parity == 0)(lambda: with_sides(odd, even_in))
    pl.when(parity == 1)(lambda: with_sides(even_in, odd))


def finish(operand, weights, rows, start, count, level, pair_of, part_sum, plane, denoised, coarse):
    def emit(slot, total):
        columns, place = columns_of(pair_of(slot), PAIR), columns_of(slot - start, PAIR)
        coarse[:, place] = total
        denoised[:, place] = part_sum[:, columns] - clip(plane[:, columns] - total, level)

    filter_columns(operand, weights, rows, start, count, emit)


def row_copies(source, target, begin, sems):
    columns = slice(begin, begin + source.shape[1])
    return [
        pltpu.make_async_copy(source.at[row : row + TILE, :], target.at[row : row + TILE, columns], sems.at[k])
        for k, row in enumerate(range(0, source.shape[0], TILE))
    ]


def coarse_one_kernel(levels, own, even_in, odd_in, part_sum, plane, high, low, denoised, coarse, flipped, operand):
    rows = own.shape[0]
    pairs = own.shape[1] // PAIR

    def blocks(one):
        def body(pair, _):
            put(one(0, 2 * pair), operand, rows, main=(pair, 0), after=pair - 1)
            put(one(0, 2 * pair + 1), operand, rows, main=(pair, 1), before=pair + 1)

        put(one(0, 1), operand, rows, before=1)
        loop(1, pairs - 1, body)
        put(one(0, 2 * pairs - 2), operand, rows, after=pairs - 2)

    with_neighbours((own,), (odd_in,), (flipped,), lambda odd: last_rows((own,), (even_in,), odd, blocks))
    finish(operand, (high, low), rows, 1, pairs - 2, levels[4:5, :], lambda slot: slot, part_sum, plane, denoised, coarse)


def coarse_two_kernel(levels, *refs):
    own, even_in, refs = refs[:2], refs[2:4], refs[4:]
    far, part_sum, plane, high, low, den_one, coa_one, denoised, coarse, *refs = refs[:2], *refs[2:]
    flipped, (operand, den_two, coa_two, den_three, coa_three, sems) = refs[:2], refs[2:]
    rows, columns = part_sum.shape
    first, pairs = own[0].shape[1] // PAIR, columns // PAIR
    begin = first - 1
    copies = row_copies(den_one, denoised, PAIR, sems.at[6]) + row_copies(coa_one, coarse, PAIR, sems.at[7])
    for copy in copies:
        copy.start()

    def blocks(one):
        def body(pair, _):
            block = 2 * (pair - first)
            put(one(1, block), operand, rows, main=(pair - begin + 1, 0), after=pair - begin)
            put(one(1, block + 1), operand, rows, main=(pair - begin + 1, 1), before=pair - begin + 2)

        loop(first, pairs, body)
        put(one(0, 2 * begin), operand, rows, main=(1, 0))
        put(one(0, 2 * begin + 1), operand, rows, main=(1, 1), before=2)
        put(one(0, 2 * begin - 1), operand, rows, before=1)
        put(one(1, 2 * (pairs - first)), operand, rows, after=pairs - begin, before=0)
        put(one(0, 0), operand, rows, main=(0, 0))
        put(one(0, 1), operand, rows, main=(0, 1))
        put(one(0, 2), operand, rows, after=0)

    with_neighbours(own, far, flipped, lambda odd: last_rows(own, even_in, odd, blocks))
    count = pairs - begin + 1
    half = count // 2
    pair_of = lambda slot: slot + begin - 1 if slot else 0
    for start, size, den, coa, at in ((0, half, den_two, coa_two, 0), (half, count - half, den_three, coa_three, 4)):
        finish(operand, (high, low), rows, start, size, levels[4:5, :], pair_of, part_sum, plane, den, coa)
        for source, target, k in ((den, denoised, at), (coa, coarse, at + 1)):
            if start == 0:
                more = row_copies(source.at[:, 0:PAIR], target, 0, sems.at[k])
                more += row_copies(source.at[:, PAIR : half * PAIR], target, begin * PAIR, sems.at[k + 2])
            else:
                more = row_copies(source, target, (begin + half - 1) * PAIR, sems.at[k])
            for copy in more:
                copy.start()
            copies += more
    for copy in copies:
        copy.wait()


def on_device(sky, thresholds):
    rows, columns = sky.shape
    row_count, col_count = lax.axis_size("rows"), lax.axis_size("cols")
    blocks, pairs = columns // LANES, columns // PAIR
    first = blocks // 2 + 6
    weights = [
        [jnp.asarray(w if k else np.concatenate([w, w])) for k, w in enumerate(column_weights(scale + 1))]
        for scale in range(SCALES)
    ]

    in_vmem = pl.BlockSpec(memory_space=pltpu.VMEM)
    any_space = pl.BlockSpec(memory_space=pl.ANY)
    in_hbm = pl.BlockSpec(memory_space=pltpu.HBM)
    dma = pltpu.SemaphoreType.DMA

    def room(mebibytes):
        return pltpu.CompilerParams(vmem_limit_bytes=mebibytes * MEBI)

    def array(width):
        return jax.ShapeDtypeStruct((rows, width), F32)

    def vmem(width):
        return pltpu.VMEM((rows, width), F32)

    def operand(slots):
        return pltpu.VMEM((slots * rows, 2 * SPAN), BF16)

    def even_swap(values):
        return lax.ppermute(values, "rows", swaps(row_count, 0))

    def odd_swap(values):
        return lax.ppermute(values, "rows", swaps(row_count, 1))

    def exchange(values):
        return even_swap(values), odd_swap(values)

    levels = jnp.broadcast_to(thresholds[:, None], (SCALES, PAIR))
    widths = (first * LANES, (blocks - first + 1) * LANES)
    part, one, two = pl.pallas_call(
        take_kernel,
        out_shape=(array(widths[0]), array(LANES), array(LANES)),
        in_specs=[in_vmem],
        out_specs=(in_vmem,) * 3,
        compiler_params=room(8),
        name="take",
    )(sky)
    near = [exchange(part)]
    one = lax.ppermute(one, "cols", swaps(col_count, 0))
    two = lax.ppermute(two, "cols", swaps(col_count, 1))
    rest = pl.pallas_call(
        join_kernel,
        out_shape=array(widths[1]),
        in_specs=[in_vmem] * 3,
        out_specs=in_vmem,
        compiler_params=room(8),
        cost_estimate=pl.CostEstimate(flops=3 * 10**10, bytes_accessed=10**6, transcendentals=0),
        name="join",
    )(sky, one, two)
    near.append(exchange(rest))
    beyond = [odd_swap(even) for even, _ in near]
    own = (part, rest)
    group = 8

    row_buffers = [pltpu.VMEM((3 * rows - cut, LANES), F32) for _ in range(group) for cut in (0, 8, 16)]

    def smooth_rows(which, name):
        width = widths[which]
        return pl.pallas_call(
            functools.partial(rows_kernel, group),
            out_shape=(array(width),) * 4,
            in_specs=[in_vmem] * 3,
            out_specs=(in_vmem,) * 4,
            scratch_shapes=[vmem(width)] + row_buffers,
            compiler_params=room(10),
            name=name,
        )(own[which], *near[which])

    smoothed = [smooth_rows(0, "rows_one"), smooth_rows(1, "rows_two")]
    four = [kept[3] for kept in smoothed]
    even_four = [even_swap(values) for values in four]

    def columnwise(pairs_of_inputs):
        return [x[0] for x in pairs_of_inputs] + [x[1] for x in pairs_of_inputs]

    fine = [w for scale in range(4) for w in weights[scale]]
    part_sum, plane = pl.pallas_call(
        functools.partial(details_kernel, pairs, tuple(len(weights[scale]) for scale in range(4))),
        out_shape=(array(columns), array(columns)),
        in_specs=[in_vmem] * (11 + len(fine)),
        out_specs=(in_vmem, in_vmem),
        scratch_shapes=[operand(pairs + 2)] * 4,
        compiler_params=room(22),
        name="details",
    )(levels, *own, *smoothed[0], *smoothed[1], *fine)

    def smooth_far(which, name, *after):
        return pl.pallas_call(
            functools.partial(far_kernel, group, len(after)),
            out_shape=array(widths[which]),
            in_specs=[in_vmem] * 3 + [any_space] * len(after),
            out_specs=in_vmem,
            scratch_shapes=row_buffers,
            compiler_params=room(10),
            name=name,
        )(near[which][1], own[which], beyond[which], *after)

    inner = first // 2 - 2
    far_one = smooth_far(0, "far_one")
    outs = pl.pallas_call(
        coarse_one_kernel,
        out_shape=(array(inner * PAIR),) * 2,
        in_specs=[in_vmem] * 8,
        out_specs=(in_vmem,) * 2,
        scratch_shapes=[vmem(widths[0]), operand(inner + 2)],
        compiler_params=room(16),
        name="coarse_one",
    )(levels, four[0], even_four[0], far_one, part_sum, plane, *weights[4])
    count = pairs - inner
    far_two = smooth_far(1, "far_two", outs[0])
    return pl.pallas_call(
        coarse_two_kernel,
        out_shape=(array(columns), array(columns)),
        in_specs=[in_vmem] * 13,
        out_specs=(in_hbm,) * 2,
        scratch_shapes=[vmem(w) for w in widths]
        + [operand(count + 2)]
        + [vmem(n * PAIR) for n in (count // 2, count // 2, count - count // 2, count - count // 2)]
        + [dma((8, rows // TILE))],
        compiler_params=room(16),
        name="coarse_two",
    )(levels, *four, *even_four, far_one, far_two, part_sum, plane, *weights[4], *outs)


def solution(mesh):
    return jax.shard_map(
        on_device,
        mesh=mesh,
        in_specs=(P("rows", "cols"), P()),
        out_specs=(P("rows", "cols"), P("rows", "cols")),
        check_vma=False,
    )
```

```python
import functools

import jax
import jax.numpy as jnp
import ml_dtypes
import numpy as np
from jax import lax
from jax.experimental import pallas as pl
from jax.experimental.pallas import tpu as pltpu
from jax.sharding import PartitionSpec as P

LANES = 128
HALF = LANES // 2
PAIR = 2 * LANES
SPAN = PAIR + LANES
TILE = 8
SCALES = 5
MEBI = 1024 * 1024
BATCH = 20
STEPS = 4
F32, BF16 = jnp.float32, jnp.bfloat16


def swaps(count, first):
    return [(i, j) for k in range(first, count - 1, 2) for i, j in ((k, k + 1), (k + 1, k))]


def column_weights(scales):
    taps = np.ones(1)
    for scale in range(scales):
        step = np.zeros(4 * 2**scale + 1)
        step[:: 2**scale] = (1.0, 4.0, 6.0, 4.0, 1.0)
        taps = np.convolve(taps, step)
    reach = len(taps) // 2
    source = np.concatenate([np.arange(PAIR + HALF), np.arange(-HALF, 0)])
    offset = source[:, None] - np.arange(PAIR)[None, :]
    exact = np.where(np.abs(offset) <= reach, taps[np.clip(offset + reach, 0, 2 * reach)], 0.0) * 2.0 ** (-8 * scales)
    high = exact.astype(ml_dtypes.bfloat16)
    low = (exact - high.astype(np.float64)).astype(ml_dtypes.bfloat16)
    return [high, low] if np.any(low.astype(np.float32)) else [high]


def binomial(a, b, c, d, e):
    return (a + e) + 4.0 * (b + d) + 6.0 * c


def columns_of(block, width=LANES):
    if isinstance(block, int):
        return slice(block * width, (block + 1) * width)
    return pl.ds(pl.multiple_of(block * width, width), width)


def loop(begin, end, body, group=1):
    def step(k, carry):
        for slot in range(group):
            body(begin + k * group + slot, slot)
        return carry

    whole = (end - begin) // group
    lax.fori_loop(0, whole, step, 0)
    for index in range(begin + whole * group, end):
        body(index, index - begin - whole * group)


def with_neighbours(own, odd_in, flipped, run, prepare=None):
    rows = own[0].shape[0]
    index, last = lax.axis_index("rows"), lax.axis_size("rows") - 1
    outer = jnp.logical_or(index == 0, index == last)

    @pl.when(outer)
    def _():
        for source, target in zip(own, flipped):
            for k in range(rows):
                target[k : k + 1, :] = source[rows - 1 - k : rows - k, :]
        run(flipped)

    @pl.when(jnp.logical_not(outer))
    def _():
        if prepare is not None:
            prepare()
        run(odd_in)


def load_block(own, even, odd, buffer):
    rows = own.shape[0]
    parity = lax.axis_index("rows") % 2
    buffer[rows : 2 * rows, :] = own
    buffer[pl.ds(pl.multiple_of((1 - parity) * 2 * rows, TILE), rows), :] = even
    buffer[pl.ds(pl.multiple_of(parity * 2 * rows, TILE), rows), :] = odd


def taps(buffer, begin, step, count):
    return [buffer[begin + k * step : begin + k * step + count, :] for k in (-2, -1, 0, 1, 2)]


def take_kernel(sky, part, first, second):
    columns = sky.shape[1]
    part[...] = sky[:, 0 : part.shape[1]]
    left, right = sky[:, 0:LANES], sky[:, columns - LANES : columns]
    even = lax.axis_index("cols") % 2 == 0
    first[...] = jnp.where(even, right, left)
    second[...] = jnp.where(even, left, right)


def join_kernel(sky, first, second, rest):
    width, columns = rest.shape[1] - LANES, sky.shape[1]
    rest[:, 0:width] = sky[:, columns - width : columns]
    rows = sky.shape[0]
    index, last = lax.axis_index("cols"), lax.axis_size("cols") - 1
    in_first = lax.broadcasted_iota(jnp.int32, (rows, LANES), 1) < HALF
    even = index % 2 == 0
    left = jnp.where(even, second[...], first[...])
    right = jnp.where(even, first[...], second[...])
    halo = slice(width, width + LANES)
    rest[:, halo] = jnp.where(in_first, right, left)

    def flip(value):
        row = lax.broadcasted_iota(jnp.int32, (LANES, LANES), 0)
        lane = lax.broadcasted_iota(jnp.int32, (LANES, LANES), 1)
        turn = (row + lane == LANES - 1).astype(F32)
        return jnp.dot(value, turn, preferred_element_type=F32, precision=lax.Precision.HIGHEST)

    @pl.when(index == 0)
    def _():
        rest[:, halo] = jnp.where(in_first, right, flip(sky[:, 0:LANES]))

    @pl.when(index == last)
    def _():
        rest[:, halo] = jnp.where(in_first, flip(sky[:, columns - LANES : columns]), left)


def smooth_tile(group, own, even_in, odd_in, out, buffers, kept=None):
    rows = own.shape[0]

    def one(block, slot):
        zero, ones, twos = buffers[3 * slot : 3 * slot + 3]
        columns = columns_of(block)
        load_block(own[:, columns], even_in[:, columns], odd_in[:, columns], zero)
        ones[...] = binomial(*taps(zero, 4, 1, 3 * rows - 8))
        two = binomial(*taps(ones, 4, 2, 3 * rows - 16))
        twos[...] = two
        n = 3 * rows - 32
        three = binomial(two[0:n], twos[4 : n + 4, :], two[8 : n + 8], twos[12 : n + 12, :], two[16 : n + 16])
        out[:, columns] = binomial(*[three[8 * k : 8 * k + rows] for k in range(5)])
        if kept is not None:
            kept[0][:, columns] = ones[rows - 4 : 2 * rows - 4, :]
            kept[1][:, columns] = two[rows - 8 : 2 * rows - 8]
            kept[2][:, columns] = three[rows - 16 : 2 * rows - 16]

    loop(0, own.shape[1] // LANES, one, group)


def rows_kernel(group, own, even_in, odd_in, ones, twos, threes, out, flipped, *buffers):
    def run(odd):
        smooth_tile(group, own, even_in, odd[0], out, buffers, (ones, twos, threes))

    with_neighbours((own,), (odd_in,), (flipped,), run)


def far_kernel(group, after, own, even_in, odd_in, *refs):
    out, *buffers = refs[after:]
    smooth_tile(group, own, even_in, odd_in, out, buffers)


def put(value, operand, rows, main=None, after=None, before=None):
    high = value.astype(BF16)
    low = (value - high.astype(F32)).astype(BF16)

    def at(slot):
        return slice(slot * rows, (slot + 1) * rows) if isinstance(slot, int) else pl.ds(pl.multiple_of(slot * rows, 16), rows)

    for base, piece in ((0, high), (SPAN, low)):
        if main is not None:
            operand[at(main[0]), base + main[1] * LANES : base + (main[1] + 1) * LANES] = piece
        if after is not None:
            operand[at(after), base + PAIR : base + PAIR + HALF] = piece[:, :HALF]
        if before is not None:
            operand[at(before), base + PAIR + HALF : base + SPAN] = piece[:, HALF:]


def clip(detail, level):
    return jnp.minimum(jnp.maximum(detail, -level), level)


def filter_columns(operand, weights, rows, start, count, emit):
    value = operand[start * rows : (start + count) * rows, :]
    total = None
    for weight in weights:
        term = jnp.dot(value[:, : weight.shape[0]], weight[...], preferred_element_type=F32)
        total = term if total is None else total + term
    for k in range(count):
        emit(start + k, total[k * rows : (k + 1) * rows])


def details_kernel(pairs, weight_counts, levels, *refs):
    own, smoothed, refs = refs[:2], (refs[2:6], refs[6:10]), refs[10:]
    weights, refs = refs[: sum(weight_counts)], refs[sum(weight_counts) :]
    out, plane, *operands = refs
    rows = own[0].shape[0]
    first = own[0].shape[1] // PAIR

    def one(span, block):
        return [values[:, columns_of(block)] for values in smoothed[span]]

    def one_pair(span, begin, pair):
        block = 2 * (pair - begin)
        left, right = one(span, block), one(span, block + 1)
        for k in range(4):
            put(left[k], operands[k], rows, main=(pair + 1, 0), after=pair)
            put(right[k], operands[k], rows, main=(pair + 1, 1), before=pair + 2)

    for k, value in enumerate(one(1, 2 * (pairs - first))):
        put(value, operands[k], rows, after=pairs, before=1)
    loop(0, first, lambda pair, slot: one_pair(0, 0, pair), 2)
    def columns_step(scale, start, count):
        def emit(slot, total):
            pair = slot - 1
            columns = columns_of(pair, PAIR)
            if scale == 0:
                sky = own[0][:, columns] if pair < first else own[1][:, columns_of(pair - first, PAIR)]
                out[:, columns] = sky - clip(sky - total, levels[scale : scale + 1, :])
            else:
                out[:, columns] = out[:, columns] - clip(plane[:, columns] - total, levels[scale : scale + 1, :])
            plane[:, columns] = total

        use = weights[sum(weight_counts[:scale]) : sum(weight_counts[: scale + 1])]
        filter_columns(operands[scale], use, rows, start + 1, count, emit)

    waiting = list(range(first, pairs))
    share = -(-len(waiting) // STEPS)
    for scale in range(4):
        for start in range(0, first - 1, BATCH):
            count = min(BATCH, first - 1 - start)
            columns_step(scale, start, count)
            for pair in waiting[:share]:
                one_pair(1, first, pair)
            waiting = waiting[share:]
    for pair in waiting:
        one_pair(1, first, pair)
    for scale in range(4):
        columns_step(scale, first - 1, pairs - first + 1)


def last_rows(own, even_in, odd, then):
    half = own[0].shape[0] // 2

    def with_sides(above, below):
        def one(span, block):
            columns = columns_of(block)
            a, b = above[span][0:half, columns], above[span][half : 2 * half, columns]
            c, d = own[span][0:half, columns], own[span][half : 2 * half, columns]
            e, f = below[span][0:half, columns], below[span][half : 2 * half, columns]
            return jnp.concatenate([binomial(a, b, c, d, e), binomial(b, c, d, e, f)], axis=0)

        then(one)

    parity = lax.axis_index("rows") % 2
    pl.when(parity == 0)(lambda: with_sides(odd, even_in))
    pl.when(parity == 1)(lambda: with_sides(even_in, odd))


def finish(operand, weights, rows, start, count, level, pair_of, part_sum, plane, denoised, coarse):
    def emit(slot, total):
        columns, place = columns_of(pair_of(slot), PAIR), columns_of(slot - start, PAIR)
        coarse[:, place] = total
        denoised[:, place] = part_sum[:, columns] - clip(plane[:, columns] - total, level)

    filter_columns(operand, weights, rows, start, count, emit)


def row_copies(source, target, begin, sems):
    columns = slice(begin, begin + source.shape[1])
    return [
        pltpu.make_async_copy(source.at[row : row + TILE, :], target.at[row : row + TILE, columns], sems.at[k])
        for k, row in enumerate(range(0, source.shape[0], TILE))
    ]


def coarse_one_kernel(levels, own, even_in, odd_in, part_sum, plane, high, low, denoised, coarse, flipped, operand):
    rows = own.shape[0]
    pairs = own.shape[1] // PAIR

    def blocks(one):
        def body(pair, _):
            put(one(0, 2 * pair), operand, rows, main=(pair, 0), after=pair - 1)
            put(one(0, 2 * pair + 1), operand, rows, main=(pair, 1), before=pair + 1)

        put(one(0, 1), operand, rows, before=1)
        loop(1, pairs - 1, body)
        put(one(0, 2 * pairs - 2), operand, rows, after=pairs - 2)

    with_neighbours((own,), (odd_in,), (flipped,), lambda odd: last_rows((own,), (even_in,), odd, blocks))
    finish(operand, (high, low), rows, 1, pairs - 2, levels[4:5, :], lambda slot: slot, part_sum, plane, denoised, coarse)


def coarse_two_kernel(levels, *refs):
    own, even_in, refs = refs[:2], refs[2:4], refs[4:]
    far, part_sum, plane, high, low, den_one, coa_one, denoised, coarse, *refs = refs[:2], *refs[2:]
    flipped, (operand, den_two, coa_two, den_three, coa_three, sems) = refs[:2], refs[2:]
    rows, columns = part_sum.shape
    first, pairs = own[0].shape[1] // PAIR, columns // PAIR
    begin = first - 1
    copies = row_copies(den_one, denoised, PAIR, sems.at[6]) + row_copies(coa_one, coarse, PAIR, sems.at[7])
    for copy in copies:
        copy.start()

    def blocks(one):
        def body(pair, _):
            block = 2 * (pair - first)
            put(one(1, block), operand, rows, main=(pair - begin + 1, 0), after=pair - begin)
            put(one(1, block + 1), operand, rows, main=(pair - begin + 1, 1), before=pair - begin + 2)

        loop(first, pairs, body)
        put(one(0, 2 * begin), operand, rows, main=(1, 0))
        put(one(0, 2 * begin + 1), operand, rows, main=(1, 1), before=2)
        put(one(0, 2 * begin - 1), operand, rows, before=1)
        put(one(1, 2 * (pairs - first)), operand, rows, after=pairs - begin, before=0)
        put(one(0, 0), operand, rows, main=(0, 0))
        put(one(0, 1), operand, rows, main=(0, 1))
        put(one(0, 2), operand, rows, after=0)

    with_neighbours(own, far, flipped, lambda odd: last_rows(own, even_in, odd, blocks))
    count = pairs - begin + 1
    half = count // 2
    pair_of = lambda slot: slot + begin - 1 if slot else 0
    for start, size, den, coa, at in ((0, half, den_two, coa_two, 0), (half, count - half, den_three, coa_three, 4)):
        finish(operand, (high, low), rows, start, size, levels[4:5, :], pair_of, part_sum, plane, den, coa)
        for source, target, k in ((den, denoised, at), (coa, coarse, at + 1)):
            if start == 0:
                more = row_copies(source.at[:, 0:PAIR], target, 0, sems.at[k])
                more += row_copies(source.at[:, PAIR : half * PAIR], target, begin * PAIR, sems.at[k + 2])
            else:
                more = row_copies(source, target, (begin + half - 1) * PAIR, sems.at[k])
            for copy in more:
                copy.start()
            copies += more
    for copy in copies:
        copy.wait()


def on_device(sky, thresholds):
    rows, columns = sky.shape
    row_count, col_count = lax.axis_size("rows"), lax.axis_size("cols")
    blocks, pairs = columns // LANES, columns // PAIR
    first = blocks // 2 + 10
    weights = [
        [jnp.asarray(w if k else np.concatenate([w, w])) for k, w in enumerate(column_weights(scale + 1))]
        for scale in range(SCALES)
    ]

    in_vmem = pl.BlockSpec(memory_space=pltpu.VMEM)
    any_space = pl.BlockSpec(memory_space=pl.ANY)
    in_hbm = pl.BlockSpec(memory_space=pltpu.HBM)
    dma = pltpu.SemaphoreType.DMA

    def room(mebibytes):
        return pltpu.CompilerParams(vmem_limit_bytes=mebibytes * MEBI)

    def array(width):
        return jax.ShapeDtypeStruct((rows, width), F32)

    def vmem(width):
        return pltpu.VMEM((rows, width), F32)

    def operand(slots):
        return pltpu.VMEM((slots * rows, 2 * SPAN), BF16)

    def even_swap(values):
        return lax.ppermute(values, "rows", swaps(row_count, 0))

    def odd_swap(values):
        return lax.ppermute(values, "rows", swaps(row_count, 1))

    def exchange(values):
        return even_swap(values), odd_swap(values)

    levels = jnp.broadcast_to(thresholds[:, None], (SCALES, PAIR))
    widths = (first * LANES, (blocks - first + 1) * LANES)
    part, one, two = pl.pallas_call(
        take_kernel,
        out_shape=(array(widths[0]), array(LANES), array(LANES)),
        in_specs=[in_vmem],
        out_specs=(in_vmem,) * 3,
        compiler_params=room(8),
        name="take",
    )(sky)
    near = [exchange(part)]
    one = lax.ppermute(one, "cols", swaps(col_count, 0))
    two = lax.ppermute(two, "cols", swaps(col_count, 1))
    rest = pl.pallas_call(
        join_kernel,
        out_shape=array(widths[1]),
        in_specs=[in_vmem] * 3,
        out_specs=in_vmem,
        compiler_params=room(8),
        cost_estimate=pl.CostEstimate(flops=3 * 10**10, bytes_accessed=10**6, transcendentals=0),
        name="join",
    )(sky, one, two)
    near.append(exchange(rest))
    beyond = [odd_swap(even) for even, _ in near]
    own = (part, rest)
    group = 8

    row_buffers = [pltpu.VMEM((3 * rows - cut, LANES), F32) for _ in range(group) for cut in (0, 8, 16)]

    def smooth_rows(which, name):
        width = widths[which]
        return pl.pallas_call(
            functools.partial(rows_kernel, group),
            out_shape=(array(width),) * 4,
            in_specs=[in_vmem] * 3,
            out_specs=(in_vmem,) * 4,
            scratch_shapes=[vmem(width)] + row_buffers,
            compiler_params=room(10),
            name=name,
        )(own[which], *near[which])

    smoothed = [smooth_rows(0, "rows_one"), smooth_rows(1, "rows_two")]
    four = [kept[3] for kept in smoothed]
    even_four = [even_swap(values) for values in four]

    def columnwise(pairs_of_inputs):
        return [x[0] for x in pairs_of_inputs] + [x[1] for x in pairs_of_inputs]

    fine = [w for scale in range(4) for w in weights[scale]]
    part_sum, plane = pl.pallas_call(
        functools.partial(details_kernel, pairs, tuple(len(weights[scale]) for scale in range(4))),
        out_shape=(array(columns), array(columns)),
        in_specs=[in_vmem] * (11 + len(fine)),
        out_specs=(in_vmem, in_vmem),
        scratch_shapes=[operand(pairs + 2)] * 4,
        compiler_params=room(22),
        name="details",
    )(levels, *own, *smoothed[0], *smoothed[1], *fine)

    def smooth_far(which, name, *after):
        return pl.pallas_call(
            functools.partial(far_kernel, group, len(after)),
            out_shape=array(widths[which]),
            in_specs=[in_vmem] * 3 + [any_space] * len(after),
            out_specs=in_vmem,
            scratch_shapes=row_buffers,
            compiler_params=room(10),
            name=name,
        )(near[which][1], own[which], beyond[which], *after)

    inner = first // 2 - 2
    far_one = smooth_far(0, "far_one")
    outs = pl.pallas_call(
        coarse_one_kernel,
        out_shape=(array(inner * PAIR),) * 2,
        in_specs=[in_vmem] * 8,
        out_specs=(in_vmem,) * 2,
        scratch_shapes=[vmem(widths[0]), operand(inner + 2)],
        compiler_params=room(16),
        name="coarse_one",
    )(levels, four[0], even_four[0], far_one, part_sum, plane, *weights[4])
    count = pairs - inner
    far_two = smooth_far(1, "far_two", outs[0])
    return pl.pallas_call(
        coarse_two_kernel,
        out_shape=(array(columns), array(columns)),
        in_specs=[in_vmem] * 13,
        out_specs=(in_hbm,) * 2,
        scratch_shapes=[vmem(w) for w in widths]
        + [operand(count + 2)]
        + [vmem(n * PAIR) for n in (count // 2, count // 2, count - count // 2, count - count // 2)]
        + [dma((8, rows // TILE))],
        compiler_params=room(16),
        name="coarse_two",
    )(levels, *four, *even_four, far_one, far_two, part_sum, plane, *weights[4], *outs)


def solution(mesh):
    return jax.shard_map(
        on_device,
        mesh=mesh,
        in_specs=(P("rows", "cols"), P()),
        out_specs=(P("rows", "cols"), P("rows", "cols")),
        check_vma=False,
    )
```

```python
import functools

import jax
import jax.numpy as jnp
import ml_dtypes
import numpy as np
from jax import lax
from jax.experimental import pallas as pl
from jax.experimental.pallas import tpu as pltpu
from jax.sharding import PartitionSpec as P

LANES = 128
HALF = LANES // 2
PAIR = 2 * LANES
SPAN = PAIR + LANES
TILE = 8
SCALES = 5
MEBI = 1024 * 1024
BATCH = 20
STEPS = 4
F32, BF16 = jnp.float32, jnp.bfloat16


def swaps(count, first):
    return [(i, j) for k in range(first, count - 1, 2) for i, j in ((k, k + 1), (k + 1, k))]


def column_weights(scales):
    taps = np.ones(1)
    for scale in range(scales):
        step = np.zeros(4 * 2**scale + 1)
        step[:: 2**scale] = (1.0, 4.0, 6.0, 4.0, 1.0)
        taps = np.convolve(taps, step)
    reach = len(taps) // 2
    source = np.concatenate([np.arange(PAIR + HALF), np.arange(-HALF, 0)])
    offset = source[:, None] - np.arange(PAIR)[None, :]
    exact = np.where(np.abs(offset) <= reach, taps[np.clip(offset + reach, 0, 2 * reach)], 0.0) * 2.0 ** (-8 * scales)
    high = exact.astype(ml_dtypes.bfloat16)
    low = (exact - high.astype(np.float64)).astype(ml_dtypes.bfloat16)
    return [high, low] if np.any(low.astype(np.float32)) else [high]


def binomial(a, b, c, d, e):
    return (a + e) + 4.0 * (b + d) + 6.0 * c


def columns_of(block, width=LANES):
    if isinstance(block, int):
        return slice(block * width, (block + 1) * width)
    return pl.ds(pl.multiple_of(block * width, width), width)


def loop(begin, end, body, group=1):
    def step(k, carry):
        for slot in range(group):
            body(begin + k * group + slot, slot)
        return carry

    whole = (end - begin) // group
    lax.fori_loop(0, whole, step, 0)
    for index in range(begin + whole * group, end):
        body(index, index - begin - whole * group)


def with_neighbours(own, odd_in, flipped, run, prepare=None):
    rows = own[0].shape[0]
    index, last = lax.axis_index("rows"), lax.axis_size("rows") - 1
    outer = jnp.logical_or(index == 0, index == last)

    @pl.when(outer)
    def _():
        for source, target in zip(own, flipped):
            for k in range(rows):
                target[k : k + 1, :] = source[rows - 1 - k : rows - k, :]
        run(flipped)

    @pl.when(jnp.logical_not(outer))
    def _():
        if prepare is not None:
            prepare()
        run(odd_in)


def load_block(own, even, odd, buffer):
    rows = own.shape[0]
    parity = lax.axis_index("rows") % 2
    buffer[rows : 2 * rows, :] = own
    buffer[pl.ds(pl.multiple_of((1 - parity) * 2 * rows, TILE), rows), :] = even
    buffer[pl.ds(pl.multiple_of(parity * 2 * rows, TILE), rows), :] = odd


def taps(buffer, begin, step, count):
    return [buffer[begin + k * step : begin + k * step + count, :] for k in (-2, -1, 0, 1, 2)]


def take_kernel(sky, part, first, second):
    columns = sky.shape[1]
    part[...] = sky[:, 0 : part.shape[1]]
    left, right = sky[:, 0:LANES], sky[:, columns - LANES : columns]
    even = lax.axis_index("cols") % 2 == 0
    first[...] = jnp.where(even, right, left)
    second[...] = jnp.where(even, left, right)


def join_kernel(sky, first, second, rest):
    width, columns = rest.shape[1] - LANES, sky.shape[1]
    rest[:, 0:width] = sky[:, columns - width : columns]
    rows = sky.shape[0]
    index, last = lax.axis_index("cols"), lax.axis_size("cols") - 1
    in_first = lax.broadcasted_iota(jnp.int32, (rows, LANES), 1) < HALF
    even = index % 2 == 0
    left = jnp.where(even, second[...], first[...])
    right = jnp.where(even, first[...], second[...])
    halo = slice(width, width + LANES)
    rest[:, halo] = jnp.where(in_first, right, left)

    def flip(value):
        row = lax.broadcasted_iota(jnp.int32, (LANES, LANES), 0)
        lane = lax.broadcasted_iota(jnp.int32, (LANES, LANES), 1)
        turn = (row + lane == LANES - 1).astype(F32)
        return jnp.dot(value, turn, preferred_element_type=F32, precision=lax.Precision.HIGHEST)

    @pl.when(index == 0)
    def _():
        rest[:, halo] = jnp.where(in_first, right, flip(sky[:, 0:LANES]))

    @pl.when(index == last)
    def _():
        rest[:, halo] = jnp.where(in_first, flip(sky[:, columns - LANES : columns]), left)


def smooth_tile(group, own, even_in, odd_in, out, buffers, kept=None):
    rows = own.shape[0]

    def one(block, slot):
        zero, ones, twos = buffers[3 * slot : 3 * slot + 3]
        columns = columns_of(block)
        load_block(own[:, columns], even_in[:, columns], odd_in[:, columns], zero)
        ones[...] = binomial(*taps(zero, 4, 1, 3 * rows - 8))
        two = binomial(*taps(ones, 4, 2, 3 * rows - 16))
        twos[...] = two
        n = 3 * rows - 32
        three = binomial(two[0:n], twos[4 : n + 4, :], two[8 : n + 8], twos[12 : n + 12, :], two[16 : n + 16])
        out[:, columns] = binomial(*[three[8 * k : 8 * k + rows] for k in range(5)])
        if kept is not None:
            kept[0][:, columns] = ones[rows - 4 : 2 * rows - 4, :]
            kept[1][:, columns] = two[rows - 8 : 2 * rows - 8]
            kept[2][:, columns] = three[rows - 16 : 2 * rows - 16]

    loop(0, own.shape[1] // LANES, one, group)


def rows_kernel(group, own, even_in, odd_in, ones, twos, threes, out, flipped, *buffers):
    def run(odd):
        smooth_tile(group, own, even_in, odd[0], out, buffers, (ones, twos, threes))

    with_neighbours((own,), (odd_in,), (flipped,), run)


def far_kernel(group, after, own, even_in, odd_in, *refs):
    out, *buffers = refs[after:]
    smooth_tile(group, own, even_in, odd_in, out, buffers)


def put(value, operand, rows, main=None, after=None, before=None):
    high = value.astype(BF16)
    low = (value - high.astype(F32)).astype(BF16)

    def at(slot):
        return slice(slot * rows, (slot + 1) * rows) if isinstance(slot, int) else pl.ds(pl.multiple_of(slot * rows, 16), rows)

    for base, piece in ((0, high), (SPAN, low)):
        if main is not None:
            operand[at(main[0]), base + main[1] * LANES : base + (main[1] + 1) * LANES] = piece
        if after is not None:
            operand[at(after), base + PAIR : base + PAIR + HALF] = piece[:, :HALF]
        if before is not None:
            operand[at(before), base + PAIR + HALF : base + SPAN] = piece[:, HALF:]


def clip(detail, level):
    return jnp.minimum(jnp.maximum(detail, -level), level)


def filter_columns(operand, weights, rows, start, count, emit):
    value = operand[start * rows : (start + count) * rows, :]
    total = None
    for weight in weights:
        term = jnp.dot(value[:, : weight.shape[0]], weight[...], preferred_element_type=F32)
        total = term if total is None else total + term
    for k in range(count):
        emit(start + k, total[k * rows : (k + 1) * rows])


def details_kernel(pairs, weight_counts, levels, *refs):
    own, smoothed, refs = refs[:2], (refs[2:6], refs[6:10]), refs[10:]
    weights, refs = refs[: sum(weight_counts)], refs[sum(weight_counts) :]
    out, plane, *operands = refs
    rows = own[0].shape[0]
    first = own[0].shape[1] // PAIR

    def one(span, block):
        return [values[:, columns_of(block)] for values in smoothed[span]]

    def one_pair(span, begin, pair):
        block = 2 * (pair - begin)
        left, right = one(span, block), one(span, block + 1)
        for k in range(4):
            put(left[k], operands[k], rows, main=(pair + 1, 0), after=pair)
            put(right[k], operands[k], rows, main=(pair + 1, 1), before=pair + 2)

    for k, value in enumerate(one(1, 2 * (pairs - first))):
        put(value, operands[k], rows, after=pairs, before=1)
    loop(0, first, lambda pair, slot: one_pair(0, 0, pair), 2)
    def columns_step(scale, start, count):
        def emit(slot, total):
            pair = slot - 1
            columns = columns_of(pair, PAIR)
            if scale == 0:
                sky = own[0][:, columns] if pair < first else own[1][:, columns_of(pair - first, PAIR)]
                out[:, columns] = sky - clip(sky - total, levels[scale : scale + 1, :])
            else:
                out[:, columns] = out[:, columns] - clip(plane[:, columns] - total, levels[scale : scale + 1, :])
            plane[:, columns] = total

        use = weights[sum(weight_counts[:scale]) : sum(weight_counts[: scale + 1])]
        filter_columns(operands[scale], use, rows, start + 1, count, emit)

    waiting = list(range(first, pairs))
    share = -(-len(waiting) // STEPS)
    for scale in range(4):
        for start in range(0, first - 1, BATCH):
            count = min(BATCH, first - 1 - start)
            columns_step(scale, start, count)
            for pair in waiting[:share]:
                one_pair(1, first, pair)
            waiting = waiting[share:]
    for pair in waiting:
        one_pair(1, first, pair)
    for scale in range(4):
        columns_step(scale, first - 1, pairs - first + 1)


def last_rows(own, even_in, odd, then):
    half = own[0].shape[0] // 2

    def with_sides(above, below):
        def one(span, block):
            columns = columns_of(block)
            a, b = above[span][0:half, columns], above[span][half : 2 * half, columns]
            c, d = own[span][0:half, columns], own[span][half : 2 * half, columns]
            e, f = below[span][0:half, columns], below[span][half : 2 * half, columns]
            return jnp.concatenate([binomial(a, b, c, d, e), binomial(b, c, d, e, f)], axis=0)

        then(one)

    parity = lax.axis_index("rows") % 2
    pl.when(parity == 0)(lambda: with_sides(odd, even_in))
    pl.when(parity == 1)(lambda: with_sides(even_in, odd))


def finish(operand, weights, rows, start, count, level, pair_of, part_sum, plane, denoised, coarse):
    def emit(slot, total):
        columns, place = columns_of(pair_of(slot), PAIR), columns_of(slot - start, PAIR)
        coarse[:, place] = total
        denoised[:, place] = part_sum[:, columns] - clip(plane[:, columns] - total, level)

    filter_columns(operand, weights, rows, start, count, emit)


def row_copies(source, target, begin, sems):
    columns = slice(begin, begin + source.shape[1])
    return [
        pltpu.make_async_copy(source.at[row : row + TILE, :], target.at[row : row + TILE, columns], sems.at[k])
        for k, row in enumerate(range(0, source.shape[0], TILE))
    ]


def coarse_one_kernel(levels, own, even_in, odd_in, part_sum, plane, high, low, denoised, coarse, flipped, operand):
    rows = own.shape[0]
    pairs = own.shape[1] // PAIR

    def blocks(one):
        def body(pair, _):
            put(one(0, 2 * pair), operand, rows, main=(pair, 0), after=pair - 1)
            put(one(0, 2 * pair + 1), operand, rows, main=(pair, 1), before=pair + 1)

        put(one(0, 1), operand, rows, before=1)
        loop(1, pairs - 1, body)
        put(one(0, 2 * pairs - 2), operand, rows, after=pairs - 2)

    with_neighbours((own,), (odd_in,), (flipped,), lambda odd: last_rows((own,), (even_in,), odd, blocks))
    finish(operand, (high, low), rows, 1, pairs - 2, levels[4:5, :], lambda slot: slot, part_sum, plane, denoised, coarse)


def coarse_two_kernel(levels, *refs):
    own, even_in, refs = refs[:2], refs[2:4], refs[4:]
    far, part_sum, plane, high, low, den_one, coa_one, denoised, coarse, *refs = refs[:2], *refs[2:]
    flipped, (operand, den_two, coa_two, den_three, coa_three, sems) = refs[:2], refs[2:]
    rows, columns = part_sum.shape
    first, pairs = own[0].shape[1] // PAIR, columns // PAIR
    begin = first - 1
    copies = row_copies(den_one, denoised, PAIR, sems.at[6]) + row_copies(coa_one, coarse, PAIR, sems.at[7])
    for copy in copies:
        copy.start()

    def blocks(one):
        def body(pair, _):
            block = 2 * (pair - first)
            put(one(1, block), operand, rows, main=(pair - begin + 1, 0), after=pair - begin)
            put(one(1, block + 1), operand, rows, main=(pair - begin + 1, 1), before=pair - begin + 2)

        loop(first, pairs, body)
        put(one(0, 2 * begin), operand, rows, main=(1, 0))
        put(one(0, 2 * begin + 1), operand, rows, main=(1, 1), before=2)
        put(one(0, 2 * begin - 1), operand, rows, before=1)
        put(one(1, 2 * (pairs - first)), operand, rows, after=pairs - begin, before=0)
        put(one(0, 0), operand, rows, main=(0, 0))
        put(one(0, 1), operand, rows, main=(0, 1))
        put(one(0, 2), operand, rows, after=0)

    with_neighbours(own, far, flipped, lambda odd: last_rows(own, even_in, odd, blocks))
    count = pairs - begin + 1
    half = 4
    pair_of = lambda slot: slot + begin - 1 if slot else 0
    for start, size, den, coa, at in ((0, half, den_two, coa_two, 0), (half, count - half, den_three, coa_three, 4)):
        finish(operand, (high, low), rows, start, size, levels[4:5, :], pair_of, part_sum, plane, den, coa)
        for source, target, k in ((den, denoised, at), (coa, coarse, at + 1)):
            if start == 0:
                more = row_copies(source.at[:, 0:PAIR], target, 0, sems.at[k])
                more += row_copies(source.at[:, PAIR : half * PAIR], target, begin * PAIR, sems.at[k + 2])
            else:
                more = row_copies(source, target, (begin + half - 1) * PAIR, sems.at[k])
            for copy in more:
                copy.start()
            copies += more
    for copy in copies:
        copy.wait()


def on_device(sky, thresholds):
    rows, columns = sky.shape
    row_count, col_count = lax.axis_size("rows"), lax.axis_size("cols")
    blocks, pairs = columns // LANES, columns // PAIR
    first = blocks // 2 + 10
    weights = [
        [jnp.asarray(w if k else np.concatenate([w, w])) for k, w in enumerate(column_weights(scale + 1))]
        for scale in range(SCALES)
    ]

    in_vmem = pl.BlockSpec(memory_space=pltpu.VMEM)
    any_space = pl.BlockSpec(memory_space=pl.ANY)
    in_hbm = pl.BlockSpec(memory_space=pltpu.HBM)
    dma = pltpu.SemaphoreType.DMA

    def room(mebibytes):
        return pltpu.CompilerParams(vmem_limit_bytes=mebibytes * MEBI)

    def array(width):
        return jax.ShapeDtypeStruct((rows, width), F32)

    def vmem(width):
        return pltpu.VMEM((rows, width), F32)

    def operand(slots):
        return pltpu.VMEM((slots * rows, 2 * SPAN), BF16)

    def even_swap(values):
        return lax.ppermute(values, "rows", swaps(row_count, 0))

    def odd_swap(values):
        return lax.ppermute(values, "rows", swaps(row_count, 1))

    def exchange(values):
        return even_swap(values), odd_swap(values)

    levels = jnp.broadcast_to(thresholds[:, None], (SCALES, PAIR))
    widths = (first * LANES, (blocks - first + 1) * LANES)
    part, one, two = pl.pallas_call(
        take_kernel,
        out_shape=(array(widths[0]), array(LANES), array(LANES)),
        in_specs=[in_vmem],
        out_specs=(in_vmem,) * 3,
        compiler_params=room(8),
        name="take",
    )(sky)
    near = [exchange(part)]
    one = lax.ppermute(one, "cols", swaps(col_count, 0))
    two = lax.ppermute(two, "cols", swaps(col_count, 1))
    rest = pl.pallas_call(
        join_kernel,
        out_shape=array(widths[1]),
        in_specs=[in_vmem] * 3,
        out_specs=in_vmem,
        compiler_params=room(8),
        cost_estimate=pl.CostEstimate(flops=3 * 10**10, bytes_accessed=10**6, transcendentals=0),
        name="join",
    )(sky, one, two)
    near.append(exchange(rest))
    beyond = [odd_swap(even) for even, _ in near]
    own = (part, rest)
    group = 8

    row_buffers = [pltpu.VMEM((3 * rows - cut, LANES), F32) for _ in range(group) for cut in (0, 8, 16)]

    def smooth_rows(which, name):
        width = widths[which]
        return pl.pallas_call(
            functools.partial(rows_kernel, group),
            out_shape=(array(width),) * 4,
            in_specs=[in_vmem] * 3,
            out_specs=(in_vmem,) * 4,
            scratch_shapes=[vmem(width)] + row_buffers,
            compiler_params=room(10),
            name=name,
        )(own[which], *near[which])

    smoothed = [smooth_rows(0, "rows_one"), smooth_rows(1, "rows_two")]
    four = [kept[3] for kept in smoothed]
    even_four = [even_swap(values) for values in four]

    def columnwise(pairs_of_inputs):
        return [x[0] for x in pairs_of_inputs] + [x[1] for x in pairs_of_inputs]

    fine = [w for scale in range(4) for w in weights[scale]]
    part_sum, plane = pl.pallas_call(
        functools.partial(details_kernel, pairs, tuple(len(weights[scale]) for scale in range(4))),
        out_shape=(array(columns), array(columns)),
        in_specs=[in_vmem] * (11 + len(fine)),
        out_specs=(in_vmem, in_vmem),
        scratch_shapes=[operand(pairs + 2)] * 4,
        compiler_params=room(22),
        name="details",
    )(levels, *own, *smoothed[0], *smoothed[1], *fine)

    def smooth_far(which, name, *after):
        return pl.pallas_call(
            functools.partial(far_kernel, group, len(after)),
            out_shape=array(widths[which]),
            in_specs=[in_vmem] * 3 + [any_space] * len(after),
            out_specs=in_vmem,
            scratch_shapes=row_buffers,
            compiler_params=room(10),
            name=name,
        )(near[which][1], own[which], beyond[which], *after)

    inner = first // 2 - 2
    far_one = smooth_far(0, "far_one")
    outs = pl.pallas_call(
        coarse_one_kernel,
        out_shape=(array(inner * PAIR),) * 2,
        in_specs=[in_vmem] * 8,
        out_specs=(in_vmem,) * 2,
        scratch_shapes=[vmem(widths[0]), operand(inner + 2)],
        compiler_params=room(16),
        name="coarse_one",
    )(levels, four[0], even_four[0], far_one, part_sum, plane, *weights[4])
    count = pairs - inner
    far_two = smooth_far(1, "far_two", outs[0])
    return pl.pallas_call(
        coarse_two_kernel,
        out_shape=(array(columns), array(columns)),
        in_specs=[in_vmem] * 13,
        out_specs=(in_hbm,) * 2,
        scratch_shapes=[vmem(w) for w in widths]
        + [operand(count + 2)]
        + [vmem(n * PAIR) for n in (4, 4, count - 4, count - 4)]
        + [dma((8, rows // TILE))],
        compiler_params=room(16),
        name="coarse_two",
    )(levels, *four, *even_four, far_one, far_two, part_sum, plane, *weights[4], *outs)


def solution(mesh):
    return jax.shard_map(
        on_device,
        mesh=mesh,
        in_specs=(P("rows", "cols"), P()),
        out_specs=(P("rows", "cols"), P("rows", "cols")),
        check_vma=False,
    )
```
